32 devices in a mesh: blk: 2 (over y), dp: 16 (over z, x, core).
Axes of the slice: x: 2, y: 2, z: 4, core: 2. Of those that a mesh axis runs over, the one named last changes fastest.
Arguments:
- inputs: bfloat16 [64, 512, 768], P('dp', 'blk'), may hold values from -6 to 6
- cotangent: bfloat16 [64, 512, 768], P('dp', 'blk'), may hold values from -6 to 6
- flags: int32 [64, 2048], P('dp', 'blk'), may hold values 0 or 1
- gain_one: float32 [768], replicated, may hold values from 0.25 to 1.75
- shift_one: float32 [768], replicated, may hold values from -1.5 to 1.5
- query_weight: bfloat16 [768, 768], replicated, may hold values from -0.21875 to 0.21875
- query_bias: float32 [768], replicated, may hold values from -1.5 to 1.5
- key_weight: bfloat16 [768, 768], replicated, may hold values from -0.21875 to 0.21875
- value_weight: bfloat16 [768, 768], replicated, may hold values from -0.21875 to 0.21875
- value_bias: float32 [768], replicated, may hold values from -1.5 to 1.5
- proj_weight: bfloat16 [768, 768], replicated, may hold values from -0.875 to 0.875
- proj_bias: float32 [768], replicated, may hold values from -1.5 to 1.5
- gain_two: float32 [768], replicated, may hold values from 0.25 to 1.75
- shift_two: float32 [768], replicated, may hold values from -1.5 to 1.5
- inner_weight: bfloat16 [768, 3072], replicated, may hold values from -0.21875 to 0.21875
- inner_bias: float32 [3072], replicated, may hold values from -1.5 to 1.5
- outer_weight: bfloat16 [3072, 768], replicated, may hold values from -0.109375 to 0.109375
- outer_bias: float32 [768], replicated, may hold values from -1.5 to 1.5
Outputs:
- output: bfloat16 [64, 512, 768], P('dp', 'blk')
- input_grad: bfloat16 [64, 512, 768], P('dp', 'blk')
- gain_one_grad: float32 [768], replicated
- shift_one_grad: float32 [768], replicated
- query_weight_grad: float32 [768, 768], replicated
- query_bias_grad: float32 [768], replicated
- key_weight_grad: float32 [768, 768], replicated
- value_weight_grad: float32 [768, 768], replicated
- value_bias_grad: float32 [768], replicated
- proj_weight_grad: float32 [768, 768], replicated
- proj_bias_grad: float32 [768], replicated
- gain_two_grad: float32 [768], replicated
- shift_two_grad: float32 [768], replicated
- inner_weight_grad: float32 [768, 3072], replicated
- inner_bias_grad: float32 [3072], replicated
- outer_weight_grad: float32 [3072, 768], replicated
- outer_bias_grad: float32 [768], replicated
The draws below stay inside these ranges and needn't reach their ends.
All inputs are finite; a program needn't handle non-finite values. No bound on the sum of `flags` on one device may be relied on, other than what follows from the above.
Results may differ from the reference program's by a relative error of at most 0.014.
Values may be sent and summed in bfloat16 or wider, within the bound.
No kernel may reach another device: no remote copies, remote signals or barrier semaphores. Data moves between devices by JAX's collectives and lax.ppermute only.
A program may use at most 256 MiB of HBM per device.

```python
import math
import jax
import jax.numpy as jnp
from jax import lax

D = 768
HEADS = 12
FF = 3072
HD = 64
STRIDE = 4
LENGTH = 512
CHARS = 2048
NROW = 64


def place_ends(entries, own_key, smallest, high):
    dims = entries.shape
    place = [jax.random.randint(jax.random.fold_in(own_key, axis), (), 0, dims[axis]) for axis in range(len(dims))]
    entries = entries.at[tuple(place)].set(smallest)
    longest = dims.index(max(dims))
    place[longest] = (place[longest] + 1) % dims[longest]
    return entries.at[tuple(place)].set(high)


def block_scale(key, dims, cuts, least, high):
    loudness, own = 1.0, jax.random.fold_in(key, 6)
    for position, blocks in cuts:
        draws = jnp.exp(jax.random.uniform(jax.random.fold_in(own, position), (blocks,), jnp.float32, least / len(cuts), high / len(cuts)))
        loudness = loudness * jnp.repeat(draws, dims[position] // blocks).reshape([-1 if axis == position else 1 for axis in range(len(dims))])
    return loudness


def scatter_about(rng, shape, width, bound, shards=(), dtype=jnp.bfloat16):
    values = jax.random.normal(rng, shape, jnp.float32) * width
    if len(shards) > 0:
        values = block_scale(rng, shape, shards, -0.22, 0.18) * values
    return jnp.clip(values, min=-bound, max=bound).astype(dtype)


def setup_inputs(seed: int = 0) -> dict:
    key_of = jax.random.split(jax.random.key(seed), 19)
    inputs = scatter_about(key_of[0], (NROW, LENGTH, D), 1.0, 6.0, ((0, 16), (1, 2)))
    cotangent = scatter_about(key_of[1], (NROW, LENGTH, D), 1.0, 6.0, ((0, 16), (1, 2)))
    flags = place_ends((jax.random.randint(key_of[2], (NROW, CHARS), 0, 20) < 3).astype(jnp.int32), jax.random.fold_in(key_of[2], 1), 0, 1)
    gain_one = jnp.clip(1.0 + 0.15 * jax.random.normal(key_of[3], (D,), jnp.float32), 0.25, 1.75)
    shift_one = scatter_about(key_of[4], (D,), 0.3, 1.5, (), jnp.float32)
    query_weight = scatter_about(key_of[5], (D, D), D ** -0.5, 0.21875)
    query_bias = scatter_about(key_of[6], (D,), 0.3, 1.5, (), jnp.float32)
    key_weight = scatter_about(key_of[7], (D, D), D ** -0.5, 0.21875)
    value_weight = scatter_about(key_of[8], (D, D), D ** -0.5, 0.21875)
    value_bias = scatter_about(key_of[9], (D,), 0.3, 1.5, (), jnp.float32)
    proj_weight = scatter_about(key_of[10], (D, D), (D // 16) ** -0.5, 0.875)
    proj_bias = scatter_about(key_of[11], (D,), 0.3, 1.5, (), jnp.float32)
    gain_two = jnp.clip(1.0 + 0.15 * jax.random.normal(key_of[12], (D,), jnp.float32), 0.25, 1.75)
    shift_two = scatter_about(key_of[13], (D,), 0.3, 1.5, (), jnp.float32)
    inner_weight = scatter_about(key_of[14], (D, FF), D ** -0.5, 0.21875)
    inner_bias = scatter_about(key_of[15], (FF,), 0.3, 1.5, (), jnp.float32)
    outer_weight = scatter_about(key_of[16], (FF, D), FF ** -0.5, 0.109375)
    outer_bias = scatter_about(key_of[17], (D,), 0.3, 1.5, (), jnp.float32)
    return dict(inputs=inputs, cotangent=cotangent, flags=flags, gain_one=gain_one, shift_one=shift_one, query_weight=query_weight, query_bias=query_bias, key_weight=key_weight, value_weight=value_weight, value_bias=value_bias, proj_weight=proj_weight, proj_bias=proj_bias, gain_two=gain_two, shift_two=shift_two, inner_weight=inner_weight, inner_bias=inner_bias, outer_weight=outer_weight, outer_bias=outer_bias)


EPS = 1e-05
HIGH = lax.Precision.HIGHEST

@jax.custom_vjp
def low(v):
    return lax.optimization_barrier(v.astype(jnp.bfloat16)).astype(jnp.float32)

@jax.custom_vjp
def low_back(v):
    return v

def low_keep(v):
    return (low(v), None)

def low_pass(kept, grad):
    return (grad,)

def back_keep(v):
    return (v, None)

def back_low(kept, grad):
    return (low(grad),)
low.defvjp(low_keep, low_pass)
low_back.defvjp(back_keep, back_low)

def normalize(values, gain, shift):
    center = values - lax.optimization_barrier(jnp.mean(values, axis=-1, keepdims=True))
    spread = lax.optimization_barrier(jnp.mean(center * center, axis=-1, keepdims=True))
    return center * lax.rsqrt(spread + EPS) * gain + shift

def project(left, weight):
    return jnp.einsum('rld,de->rle', left, weight, precision=HIGH)

def forward(params, hidden):
    gain_one, shift_one, query_weight, query_bias, key_weight, value_weight, value_bias, proj_weight, proj_bias, gain_two, shift_two, inner_weight, inner_bias, outer_weight, outer_bias = params
    batch = hidden.shape[0]
    first = low(normalize(hidden, gain_one, shift_one))
    query = low_back(low(project(first, query_weight) + query_bias)).reshape(batch, LENGTH, HEADS, HD)
    key = low_back(low(project(first, key_weight))).reshape(batch, LENGTH, HEADS, HD)
    value = low_back(low(project(first, value_weight) + value_bias)).reshape(batch, LENGTH, HEADS, HD)
    scores = low_back(jnp.einsum('rqhc,rkhc->rhqk', query, key, precision=HIGH) * HD ** (-0.5))
    weights = jnp.exp(scores - lax.optimization_barrier(jnp.max(scores, axis=-1, keepdims=True)))
    probs = low(weights / lax.optimization_barrier(jnp.sum(weights, axis=-1, keepdims=True)))
    mixed = jnp.einsum('rhqk,rkhc->rqhc', probs, value, precision=HIGH).reshape(batch, LENGTH, D)
    mixed = low_back(low(mixed))
    resid = hidden + low_back(project(mixed, proj_weight) + proj_bias)
    second = low(normalize(resid, gain_two, shift_two))
    inner = low_back(project(second, inner_weight) + inner_bias)
    act = low(jax.nn.gelu(inner, approximate=False))
    return resid + project(act, outer_weight) + outer_bias

def reference(inputs, cotangent, flags, gain_one, shift_one, query_weight, query_bias, key_weight, value_weight, value_bias, proj_weight, proj_bias, gain_two, shift_two, inner_weight, inner_bias, outer_weight, outer_bias):
    params = tuple((item.astype(jnp.float32) for item in (gain_one, shift_one, query_weight, query_bias, key_weight, value_weight, value_bias, proj_weight, proj_bias, gain_two, shift_two, inner_weight, inner_bias, outer_weight, outer_bias)))
    group = math.gcd(NROW, max(1, 4096 // LENGTH))
    blocks = NROW // group
    masked = lax.optimization_barrier(jnp.max(flags.reshape(NROW, LENGTH, STRIDE), axis=-1)).astype(jnp.float32)
    grad_out = cotangent.astype(jnp.float32) * masked[:, :, None]
    hidden = inputs.astype(jnp.float32).reshape(blocks, group, LENGTH, D)
    grad_out = grad_out.reshape(blocks, group, LENGTH, D)

    def step(totals, pair):
        block, block_grad = pair
        result, pull = jax.vjp(forward, params, block)
        param_grads, input_part = pull(block_grad)
        totals = jax.tree.map(jnp.add, totals, param_grads)
        return (totals, (result.astype(jnp.bfloat16), input_part.astype(jnp.bfloat16)))
    start = tuple((jnp.zeros_like(item) for item in params))
    totals, (results, input_parts) = lax.scan(step, start, (hidden, grad_out))
    return (results.reshape(NROW, LENGTH, D), input_parts.reshape(NROW, LENGTH, D), totals[0], totals[1], totals[2], totals[3], totals[4], totals[5], totals[6], totals[7], totals[8], totals[9], totals[10], totals[11], totals[12], totals[13], totals[14])
```

```python
import functools
import jax
import jax.numpy as jnp
from jax import lax
from jax.experimental import pallas as pl
from jax.experimental.pallas import tpu as pltpu
from jax.sharding import PartitionSpec as P

HEADS = 12
EPS = 1e-05
F32 = jnp.float32
BF16 = jnp.bfloat16
PAIR = 128
VMEM = 56 * 1024 * 1024
ROOT_HALF = 0.7071067811865476
ROOT_TWO_PI = 0.3989422804014327


def params(steps):
    return pltpu.CompilerParams(
        dimension_semantics=("arbitrary",) * steps, vmem_limit_bytes=VMEM
    )


def dot(left, right):
    return lax.dot_general(left, right, (((1,), (0,)), ((), ())), preferred_element_type=F32)


def dot_nt(left, right):
    return lax.dot_general(left, right, (((1,), (1,)), ((), ())), preferred_element_type=F32)


def dot_tn(left, right):
    return lax.dot_general(left, right, (((0,), (0,)), ((), ())), preferred_element_type=F32)


def normalize(values):
    center = values - jnp.mean(values, axis=-1, keepdims=True)
    scale = lax.rsqrt(jnp.mean(center * center, axis=-1, keepdims=True) + EPS)
    return center * scale, scale


def norm_back(grad, unit, scale, gain):
    scaled = grad * gain
    return scale * (
        scaled
        - jnp.mean(scaled, axis=-1, keepdims=True)
        - unit * jnp.mean(scaled * unit, axis=-1, keepdims=True)
    )


def column_sum(values):
    return jnp.sum(values, axis=0, keepdims=True)


def qkv_kernel(x_ref, gain, shift, wq, wk, wv, bq, bv, first_ref, q_ref, k_ref, v_ref):
    unit, _ = normalize(x_ref[...].astype(F32))
    first = (unit * gain[...] + shift[...]).astype(BF16)
    first_ref[...] = first
    q_ref[...] = ((dot(first, wq[...]) + bq[...]).astype(BF16).astype(F32) * 0.125).astype(BF16)
    k_ref[...] = dot(first, wk[...]).astype(BF16)
    v_ref[...] = (dot(first, wv[...]) + bv[...]).astype(BF16)


def qkv_call(x, gain, shift, wq, wk, wv, bq, bv, tile=256):
    tokens, width = x.shape
    tile_spec = pl.BlockSpec((tile, width), lambda i: (i, 0))
    vec = pl.BlockSpec((1, width), lambda i: (0, 0))
    mat = pl.BlockSpec((width, width), lambda i: (0, 0))
    out = jax.ShapeDtypeStruct((tokens, width), BF16)
    return pl.pallas_call(
        qkv_kernel,
        grid=(tokens // tile,),
        in_specs=[tile_spec, vec, vec, mat, mat, mat, vec, vec],
        out_specs=[tile_spec] * 4,
        out_shape=[out] * 4,
        compiler_params=params(1),
        cost_estimate=pl.CostEstimate(
            flops=6 * tokens * width * width, bytes_accessed=10 * tokens * width, transcendentals=0
        ),
        name="qkv",
    )(x, gain, shift, wq, wk, wv, bq, bv)


def head_masks():
    lane = lax.broadcasted_iota(jnp.int32, (1, PAIR), 1)
    low = (lane < PAIR // 2).astype(F32)
    return low, 1.0 - low


def masked(values, mask):
    return (values.astype(F32) * mask).astype(BF16)


def attention_kernel(q_ref, k_ref, v_ref, mixed_ref, probs_ref):
    length = 2 * q_ref.shape[2]
    q = q_ref[...].reshape(length, PAIR)
    k = k_ref[...].reshape(length, PAIR)
    v = v_ref[...].reshape(length, PAIR)
    total = None
    for head, mask in enumerate(head_masks()):
        scores = dot_nt(masked(q, mask), k)
        weights = jnp.exp(scores - jnp.max(scores, axis=-1, keepdims=True))
        probs = (weights * (1.0 / jnp.sum(weights, axis=-1, keepdims=True))).astype(BF16)
        probs_ref[0, head] = probs
        part = dot(probs, masked(v, mask))
        total = part if total is None else total + part
    mixed_ref[...] = total.astype(BF16).reshape(mixed_ref.shape)


def attention_call(q, k, v):
    halves, rows, half, width = q.shape
    pairs = width // PAIR
    length = 2 * half
    spec = pl.BlockSpec((2, 1, half, PAIR), lambda r, p: (0, r, 0, p))
    return pl.pallas_call(
        attention_kernel,
        grid=(rows, pairs),
        in_specs=[spec] * 3,
        out_specs=[
            spec,
            pl.BlockSpec((1, 2, length, length), lambda r, p: (r * pairs + p, 0, 0, 0)),
        ],
        out_shape=[
            jax.ShapeDtypeStruct(q.shape, BF16),
            jax.ShapeDtypeStruct((rows * pairs, 2, length, length), BF16),
        ],
        compiler_params=params(2),
        cost_estimate=pl.CostEstimate(
            flops=16 * rows * length * length * width,
            bytes_accessed=8 * rows * length * width + 4 * rows * pairs * length * length,
            transcendentals=rows * 2 * pairs * length * length,
        ),
        name="attention",
    )(q, k, v)


def attention_back_kernel(q_ref, k_ref, v_ref, mixed_ref, grad_ref, probs_ref, dq_ref, dk_ref, dv_ref):
    length = 2 * q_ref.shape[2]
    q = q_ref[...].reshape(length, PAIR)
    k = k_ref[...].reshape(length, PAIR)
    v = v_ref[...].reshape(length, PAIR)
    grad = grad_ref[...].reshape(length, PAIR)
    mixed = mixed_ref[...].reshape(length, PAIR)
    dots = grad.astype(F32) * mixed.astype(F32)
    dq = dk = dv = None
    for head, mask in enumerate(head_masks()):
        own = masked(grad, mask)
        probs = probs_ref[0, head]
        grad_probs = dot_nt(own, v)
        delta = jnp.sum(dots * mask, axis=-1, keepdims=True)
        scores = (probs.astype(F32) * (grad_probs - delta)).astype(BF16)
        part_v = dot_tn(probs, own)
        part_q = dot(scores, masked(k, mask))
        part_k = dot_tn(scores, masked(q, mask))
        dq = part_q if dq is None else dq + part_q
        dk = part_k if dk is None else dk + part_k
        dv = part_v if dv is None else dv + part_v
    dq_ref[...] = (dq * 0.125).astype(BF16).reshape(dq_ref.shape)
    dk_ref[...] = dk.astype(BF16).reshape(dk_ref.shape)
    dv_ref[...] = dv.astype(BF16).reshape(dv_ref.shape)


def attention_back_call(q, k, v, mixed, grad, probs):
    halves, rows, half, width = q.shape
    pairs = width // PAIR
    length = 2 * half
    spec = pl.BlockSpec((2, 1, half, PAIR), lambda r, p: (0, r, 0, p))
    return pl.pallas_call(
        attention_back_kernel,
        grid=(rows, pairs),
        in_specs=[spec] * 5
        + [pl.BlockSpec((1, 2, length, length), lambda r, p: (r * pairs + p, 0, 0, 0))],
        out_specs=[spec] * 3,
        out_shape=[jax.ShapeDtypeStruct(q.shape, BF16)] * 3,
        compiler_params=params(2),
        cost_estimate=pl.CostEstimate(
            flops=32 * rows * length * length * width,
            bytes_accessed=16 * rows * length * width + 4 * rows * pairs * length * length,
            transcendentals=0,
        ),
        name="attention_back",
    )(q, k, v, mixed, grad, probs)


def proj_kernel(mixed_ref, x_ref, w, b, gain, shift, resid_ref, second_ref):
    resid = x_ref[...].astype(F32) + (dot(mixed_ref[...], w[...]) + b[...])
    resid_ref[...] = resid
    unit, _ = normalize(resid)
    second_ref[...] = (unit * gain[...] + shift[...]).astype(BF16)


def proj_call(mixed, x, w, b, gain, shift, tile=256):
    tokens, width = x.shape
    tile_spec = pl.BlockSpec((tile, width), lambda i: (i, 0))
    vec = pl.BlockSpec((1, width), lambda i: (0, 0))
    mat = pl.BlockSpec((width, width), lambda i: (0, 0))
    return pl.pallas_call(
        proj_kernel,
        grid=(tokens // tile,),
        in_specs=[tile_spec, tile_spec, mat, vec, vec, vec],
        out_specs=[tile_spec] * 2,
        out_shape=[
            jax.ShapeDtypeStruct((tokens, width), F32),
            jax.ShapeDtypeStruct((tokens, width), BF16),
        ],
        compiler_params=params(1),
        cost_estimate=pl.CostEstimate(
            flops=2 * tokens * width * width, bytes_accessed=10 * tokens * width, transcendentals=0
        ),
        name="proj",
    )(mixed, x, w, b, gain, shift)


def ffn_kernel(tile, start, last, second_ref, grad_ref, w_in, b_in, w_out, base_ref, more_ref, b_out,
               out_ref, gs_ref, dw_ref, dbias_ref, acc, gacc, din_acc, dout_acc):
    step = pl.program_id(0)
    steps = pl.num_programs(0)
    tokens = second_ref.shape[0]

    @pl.when(step == 0)
    def _():
        acc[...] = base_ref[...]
        if start:
            gacc[...] = jnp.zeros_like(gacc)
        else:
            gacc[...] = more_ref[...]

    def body(i, total):
        rows = pl.ds(pl.multiple_of(i * tile, tile), tile)
        second = second_ref[rows, :]
        grad = grad_ref[rows, :]
        inner = dot(second, w_in[...]) + b_in[...]
        dact = dot_nt(grad, w_out[...])
        phi = 0.5 * (1.0 + lax.erf(inner * ROOT_HALF))
        act = (inner * phi).astype(BF16)
        slope = phi + inner * jnp.exp(-0.5 * inner * inner) * ROOT_TWO_PI
        ginner = (dact * slope).astype(BF16)
        acc[rows, :] += dot(act, w_out[...])
        gacc[rows, :] += dot_nt(ginner, w_in[...])
        part_out = dot_tn(act, grad)
        part_in = dot_tn(second, ginner)

        @pl.when(i == 0)
        def _():
            dout_acc[...] = part_out
            din_acc[...] = part_in

        @pl.when(i > 0)
        def _():
            dout_acc[...] += part_out
            din_acc[...] += part_in

        return total + column_sum(ginner.astype(F32))

    total = lax.fori_loop(0, tokens // tile, body, jnp.zeros((1, w_in.shape[1]), F32))
    dbias_ref[...] = total
    dw_ref[0, 0] = din_acc[...].astype(BF16)
    dw_ref[0, 1] = dout_acc[...].astype(BF16)

    @pl.when(step == steps - 1)
    def _():
        if last:
            out_ref[...] = (acc[...] + b_out[...]).astype(BF16)
        else:
            out_ref[...] = acc[...]
        gs_ref[...] = gacc[...]


def ffn_call(second, grad, w_in, b_in, w_out, base, more, b_out, lower, upper, chunk, start, last, tile=512):
    tokens, width = second.shape
    steps = (upper - lower) // chunk
    skip = lower // chunk
    whole = pl.BlockSpec((tokens, width), lambda j: (0, 0))
    vec = pl.BlockSpec((1, width), lambda j: (0, 0))
    more_spec = vec if start else whole
    return pl.pallas_call(
        functools.partial(ffn_kernel, tile, start, last),
        grid=(steps,),
        in_specs=[
            whole,
            whole,
            pl.BlockSpec((width, chunk), lambda j: (0, j + skip)),
            pl.BlockSpec((1, chunk), lambda j: (0, j + skip)),
            pl.BlockSpec((chunk, width), lambda j: (j + skip, 0)),
            whole,
            more_spec,
            vec,
        ],
        out_specs=[
            whole,
            whole,
            pl.BlockSpec((1, 2, width, chunk), lambda j: (j, 0, 0, 0)),
            pl.BlockSpec((1, chunk), lambda j: (0, j)),
        ],
        out_shape=[
            jax.ShapeDtypeStruct((tokens, width), BF16 if last else F32),
            jax.ShapeDtypeStruct((tokens, width), F32),
            jax.ShapeDtypeStruct((steps, 2, width, chunk), BF16),
            jax.ShapeDtypeStruct((1, upper - lower), F32),
        ],
        scratch_shapes=[
            pltpu.VMEM((tokens, width), F32),
            pltpu.VMEM((tokens, width), F32),
            pltpu.VMEM((width, chunk), F32),
            pltpu.VMEM((chunk, width), F32),
        ],
        compiler_params=params(1),
        cost_estimate=pl.CostEstimate(
            flops=12 * tokens * width * (upper - lower),
            bytes_accessed=20 * tokens * width + 8 * width * (upper - lower),
            transcendentals=2 * tokens * (upper - lower),
        ),
        name="ffn",
    )(second, grad, w_in, b_in, w_out, base, more, b_out)


def proj_back_kernel(gs_ref, resid_ref, grad_ref, mixed_ref, w, gain,
                     gresid_ref, gmixed_ref, dw_ref, vec_ref, dw_acc, vec_acc):
    step = pl.program_id(0)
    steps = pl.num_programs(0)
    unit, scale = normalize(resid_ref[...])
    gs = gs_ref[...]
    grad = grad_ref[...].astype(F32)
    gresid = grad + norm_back(gs, unit, scale, gain[...])
    gresid_ref[...] = gresid
    branch = gresid.astype(BF16)
    gmixed_ref[...] = dot_nt(branch, w[...]).astype(BF16)
    part = dot_tn(mixed_ref[...], branch)
    sums = jnp.concatenate(
        [
            column_sum(gs * unit),
            column_sum(gs),
            column_sum(branch.astype(F32)),
            column_sum(grad),
            jnp.zeros((4, gs.shape[1]), F32),
        ],
        axis=0,
    )

    @pl.when(step == 0)
    def _():
        dw_acc[...] = part
        vec_acc[...] = sums

    @pl.when(step > 0)
    def _():
        dw_acc[...] += part
        vec_acc[...] += sums

    @pl.when(step == steps - 1)
    def _():
        dw_ref[...] = dw_acc[...].astype(BF16)
        vec_ref[...] = vec_acc[...]


def proj_back_call(gs, resid, grad, mixed, w, gain, tile=256):
    tokens, width = resid.shape
    tile_spec = pl.BlockSpec((tile, width), lambda i: (i, 0))
    vec = pl.BlockSpec((1, width), lambda i: (0, 0))
    mat = pl.BlockSpec((width, width), lambda i: (0, 0))
    return pl.pallas_call(
        proj_back_kernel,
        grid=(tokens // tile,),
        in_specs=[tile_spec] * 4 + [mat, vec],
        out_specs=[tile_spec, tile_spec, mat, pl.BlockSpec((8, width), lambda i: (0, 0))],
        out_shape=[
            jax.ShapeDtypeStruct((tokens, width), F32),
            jax.ShapeDtypeStruct((tokens, width), BF16),
            jax.ShapeDtypeStruct((width, width), BF16),
            jax.ShapeDtypeStruct((8, width), F32),
        ],
        scratch_shapes=[pltpu.VMEM((width, width), F32), pltpu.VMEM((8, width), F32)],
        compiler_params=params(1),
        cost_estimate=pl.CostEstimate(
            flops=4 * tokens * width * width, bytes_accessed=18 * tokens * width, transcendentals=0
        ),
        name="proj_back",
    )(gs, resid, grad, mixed, w, gain)


def qkv_back_kernel(dq_ref, dk_ref, dv_ref, first_ref, x_ref, gresid_ref, wq, wk, wv, gain,
                    gin_ref, dw_ref, vec_ref, dw_acc, vec_acc):
    step = pl.program_id(0)
    steps = pl.num_programs(0)
    dq, dk, dv, first = dq_ref[...], dk_ref[...], dv_ref[...], first_ref[...]
    gfirst = dot_nt(dq, wq[...]) + dot_nt(dk, wk[...]) + dot_nt(dv, wv[...])
    unit, scale = normalize(x_ref[...].astype(F32))
    gin_ref[...] = (gresid_ref[...] + norm_back(gfirst, unit, scale, gain[...])).astype(BF16)
    parts = [dot_tn(first, part) for part in (dq, dk, dv)]
    sums = jnp.concatenate(
        [
            column_sum(gfirst * unit),
            column_sum(gfirst),
            column_sum(dq.astype(F32)),
            column_sum(dv.astype(F32)),
            jnp.zeros((4, first.shape[1]), F32),
        ],
        axis=0,
    )

    @pl.when(step == 0)
    def _():
        for n, part in enumerate(parts):
            dw_acc[n] = part
        vec_acc[...] = sums

    @pl.when(step > 0)
    def _():
        for n, part in enumerate(parts):
            dw_acc[n] += part
        vec_acc[...] += sums

    @pl.when(step == steps - 1)
    def _():
        dw_ref[...] = dw_acc[...].astype(BF16)
        vec_ref[...] = vec_acc[...]


def qkv_back_call(dq, dk, dv, first, x, gresid, wq, wk, wv, gain, tile=256):
    tokens, width = x.shape
    tile_spec = pl.BlockSpec((tile, width), lambda i: (i, 0))
    vec = pl.BlockSpec((1, width), lambda i: (0, 0))
    mat = pl.BlockSpec((width, width), lambda i: (0, 0))
    return pl.pallas_call(
        qkv_back_kernel,
        grid=(tokens // tile,),
        in_specs=[tile_spec] * 6 + [mat] * 3 + [vec],
        out_specs=[
            tile_spec,
            pl.BlockSpec((3, width, width), lambda i: (0, 0, 0)),
            pl.BlockSpec((8, width), lambda i: (0, 0)),
        ],
        out_shape=[
            jax.ShapeDtypeStruct((tokens, width), BF16),
            jax.ShapeDtypeStruct((3, width, width), BF16),
            jax.ShapeDtypeStruct((8, width), F32),
        ],
        scratch_shapes=[pltpu.VMEM((3, width, width), F32), pltpu.VMEM((8, width), F32)],
        compiler_params=params(1),
        cost_estimate=pl.CostEstimate(
            flops=12 * tokens * width * width, bytes_accessed=20 * tokens * width, transcendentals=0
        ),
        name="qkv_back",
    )(dq, dk, dv, first, x, gresid, wq, wk, wv, gain)


def swap(values, hop):
    axis, bit, size = hop
    pairs = [(i, i ^ bit) for i in range(size)]
    return lax.ppermute(values, axis, pairs)


def side_of(hop):
    axis, bit, _ = hop
    return (lax.axis_index(axis) // bit) % 2


def reduce_hop(values, hop):
    half = values.shape[0] // 2
    side = side_of(hop)
    kept = lax.dynamic_slice_in_dim(values, side * half, half, 0)
    sent = lax.dynamic_slice_in_dim(values, (1 - side) * half, half, 0)
    return (kept.astype(F32) + swap(sent, hop).astype(F32)).astype(BF16)


def gather_hop(values, hop):
    other = swap(values, hop)
    side = side_of(hop)
    return jnp.concatenate(
        [jnp.where(side == 0, values, other), jnp.where(side == 0, other, values)], axis=0
    )


def sum_over_devices(values, hops):
    for hop in hops:
        values = reduce_hop(values, hop)
    for hop in reversed(hops):
        values = gather_hop(values, hop)
    return values


def on_device(
    sizes,
    inputs,
    cotangent,
    flags,
    gain_one,
    shift_one,
    query_weight,
    query_bias,
    key_weight,
    value_weight,
    value_bias,
    proj_weight,
    proj_bias,
    gain_two,
    shift_two,
    inner_weight,
    inner_bias,
    outer_weight,
    outer_bias,
):
    batch, half, width = inputs.shape
    hidden = inner_weight.shape[1]
    rows = batch // 2
    blk_hop = ("blk", 1, sizes["blk"])
    bits = [1 << n for n in range(sizes["dp"].bit_length() - 1)]
    dp_hops = [("dp", bit, sizes["dp"]) for bit in bits]
    hops = dp_hops[:2] + [blk_hop] + dp_hops[2:]

    def row(vector):
        return vector.reshape(1, -1)

    masked_flags = jnp.max(flags.reshape(batch, half, -1), axis=-1)
    grad_low = jnp.where(masked_flags[:, :, None] > 0, cotangent, jnp.zeros_like(cotangent))
    mine = lax.axis_index("blk") * rows
    theirs = (1 - lax.axis_index("blk")) * rows

    def both_halves(values):
        kept = lax.dynamic_slice_in_dim(values, mine, rows, 0)
        sent = lax.dynamic_slice_in_dim(values, theirs, rows, 0)
        return jnp.concatenate([kept, swap(sent, blk_hop)], axis=0).reshape(batch * half, width)

    def home(values):
        values = values.reshape(2, rows, half, width)
        back = swap(values[1], blk_hop)
        side = side_of(blk_hop)
        return jnp.concatenate(
            [jnp.where(side == 0, values[0], back), jnp.where(side == 0, back, values[0])], axis=0
        )

    x = both_halves(inputs)
    grad = both_halves(grad_low)
    first, q, k, v = qkv_call(
        x, row(gain_one), row(shift_one), query_weight, key_weight, value_weight,
        row(query_bias), row(value_bias),
    )
    grouped = (2, rows, half, width)
    q, k, v = (t.reshape(grouped) for t in (q, k, v))
    mixed, probs = attention_call(q, k, v)
    mixed_flat = mixed.reshape(x.shape)
    resid, second = proj_call(
        mixed_flat, x, proj_weight, row(proj_bias), row(gain_two), row(shift_two)
    )
    middle = hidden // 2
    chunk = width
    out_part, gs_part, blocks_one, bias_one = ffn_call(
        second, grad, inner_weight, row(inner_bias), outer_weight, resid, row(gain_one),
        row(outer_bias), 0, middle, chunk, True, False,
    )
    out, gs, blocks_two, bias_two = ffn_call(
        second, grad, inner_weight, row(inner_bias), outer_weight, out_part, gs_part,
        row(outer_bias), middle, hidden, chunk, False, True,
    )
    gresid, gmixed, dw_proj, vec_two = proj_back_call(
        gs, resid, grad, mixed_flat, proj_weight, row(gain_two)
    )
    dq, dk, dv = attention_back_call(q, k, v, mixed, gmixed.reshape(grouped), probs)
    dq, dk, dv = (t.reshape(x.shape) for t in (dq, dk, dv))
    gin, dw_qkv, vec_one = qkv_back_call(
        dq, dk, dv, first, x, gresid, query_weight, key_weight, value_weight, row(gain_one)
    )
    output = home(out)
    input_grad = home(gin)

    vectors = jnp.concatenate(
        [vec_one[0:4].reshape(-1), vec_two[0:4].reshape(-1), bias_one.reshape(-1), bias_two.reshape(-1)]
    )
    vectors = lax.psum(vectors, ("blk", "dp"))
    gain_one_grad, shift_one_grad, query_bias_grad, value_bias_grad = (
        vectors[n * width : (n + 1) * width] for n in range(4)
    )
    gain_two_grad, shift_two_grad, proj_bias_grad, outer_bias_grad = (
        vectors[n * width : (n + 1) * width] for n in range(4, 8)
    )
    inner_bias_grad = vectors[8 * width :]

    def square(values):
        return values.reshape(-1, width, width)

    one = square(sum_over_devices(blocks_one.reshape(-1, width), hops))
    two = square(sum_over_devices(blocks_two.reshape(-1, width), hops))
    rest = jnp.concatenate([dw_proj, dw_qkv.reshape(-1, width)], axis=0)
    rest = square(sum_over_devices(rest, hops)).astype(F32)
    steps = middle // chunk
    inner_weight_grad = jnp.concatenate(
        [one[2 * n] for n in range(steps)] + [two[2 * n] for n in range(steps)], axis=1
    ).astype(F32)
    outer_weight_grad = jnp.concatenate(
        [one[2 * n + 1] for n in range(steps)] + [two[2 * n + 1] for n in range(steps)], axis=0
    ).astype(F32)
    return (
        output,
        input_grad,
        gain_one_grad,
        shift_one_grad,
        rest[1],
        query_bias_grad,
        rest[2],
        rest[3],
        value_bias_grad,
        rest[0],
        proj_bias_grad,
        gain_two_grad,
        shift_two_grad,
        inner_weight_grad,
        inner_bias_grad,
        outer_weight_grad,
        outer_bias_grad,
    )


def solution(mesh):
    sizes = dict(mesh.shape)
    split = P("dp", "blk", None)
    in_specs = (split, split, P("dp", "blk")) + (P(),) * 15
    out_specs = (split, split) + (P(),) * 15
    return jax.shard_map(
        functools.partial(on_device, sizes),
        mesh=mesh,
        in_specs=in_specs,
        out_specs=out_specs,
        check_vma=False,
    )
```

```python
import functools
import math

import jax
import jax.numpy as jnp
from jax import lax
from jax.experimental import pallas as pl
from jax.experimental.pallas import tpu as pltpu
from jax.sharding import Mesh, PartitionSpec as P

EPS = 1e-05
F32 = jnp.float32
BF16 = jnp.bfloat16
PAIR = 128
MIB = 1024 * 1024
ROOT_HALF = 0.7071067811865476
ROOT_TWO_PI = 0.3989422804014327
VM = pl.BlockSpec(memory_space=pltpu.VMEM)
TILES = 2
FFN_LIMIT = 15


def dot(left, right):
    return lax.dot_general(left, right, (((1,), (0,)), ((), ())), preferred_element_type=F32)


def dot_nt(left, right):
    return lax.dot_general(left, right, (((1,), (1,)), ((), ())), preferred_element_type=F32)


def dot_tn(left, right):
    return lax.dot_general(left, right, (((0,), (0,)), ((), ())), preferred_element_type=F32)


def normalize(values):
    center = values - jnp.mean(values, axis=-1, keepdims=True)
    scale = lax.rsqrt(jnp.mean(center * center, axis=-1, keepdims=True) + EPS)
    return center * scale, scale


def norm_back(grad, unit, scale, gain):
    scaled = grad * gain
    return scale * (
        scaled
        - jnp.mean(scaled, axis=-1, keepdims=True)
        - unit * jnp.mean(scaled * unit, axis=-1, keepdims=True)
    )


def both(one_ref, two_ref):
    return jnp.concatenate([one_ref[...], two_ref[...]], axis=0)


def four(own_ref, other_ref):
    return jnp.concatenate([own_ref[0], other_ref[0], own_ref[1], other_ref[1]], axis=0)


def column_sum(values):
    return jnp.sum(values.astype(F32), axis=0, keepdims=True)


def shape(dims, dtype):
    return jax.ShapeDtypeStruct(dims, dtype)


class Chain:
    def __init__(self):
        self.token = jnp.zeros((8, PAIR), F32)


CHAIN = []
SHARE = 10
ADD_SLOPE = 2.0
BYTES = 200.0


def cost_of(us):
    flops, size = int(us * SHARE * 1.15e9), int(us * BYTES * 3.3e6)
    return pl.CostEstimate(flops=flops, bytes_accessed=size, transcendentals=0)


def kernel_call(body, name, outs, operands, limit, us, aliases=(), scalars=0, cut=None):
    chain = CHAIN[-1]
    count = len(operands)

    def whole(*refs):
        body(*refs[:count], *refs[count + 1 : -1])
        refs[-1][...] = jnp.zeros((8, PAIR), F32)

    specs = [pl.BlockSpec(memory_space=pltpu.SMEM)] * scalars + [VM] * (count + 1 - scalars)
    for place, spec in (cut or {}).items():
        specs[place] = spec
    results = pl.pallas_call(
        whole,
        grid=(1,) if cut else (),
        in_specs=specs,
        out_specs=[VM] * (len(outs) + 1),
        out_shape=list(outs) + [shape((8, PAIR), F32)],
        input_output_aliases=dict(aliases),
        compiler_params=pltpu.CompilerParams(vmem_limit_bytes=limit * MIB),
        cost_estimate=cost_of(us),
        name=name,
    )(*operands, chain.token)
    chain.token = results[-1]
    return results[:-1]


def qkv_kernel(own_ref, other_ref, gain, shift, wq, wk, wv, bq, bv, q_ref, k_ref, v_ref):
    unit, _ = normalize(both(own_ref, other_ref).astype(F32))
    first = (unit * gain[...] + shift[...]).astype(BF16)
    q_ref[...] = ((dot(first, wq[...]) + bq[...]).astype(BF16).astype(F32) * 0.125).astype(BF16)
    k_ref[...] = dot(first, wk[...]).astype(BF16)
    v_ref[...] = (dot(first, wv[...]) + bv[...]).astype(BF16)


def qkv_call(own, other, *weights):
    half, width = own.shape
    outs = [shape((2 * half, width), BF16)] * 3
    return kernel_call(
        qkv_kernel, "qkv", outs, (own, other) + weights, 16, 3.0
    )


def mask_kernel(sent_ref, kept_ref, sent_flags, kept_flags, sent_out, kept_out):
    for values, flags, out in ((sent_ref, sent_flags, sent_out), (kept_ref, kept_flags, kept_out)):
        keep = jnp.max(flags[...], axis=-1, keepdims=True)
        out[...] = (values[...].astype(F32) * keep.astype(F32)).astype(BF16)


def mask_call(sent, kept, sent_flags, kept_flags):
    outs = [shape(sent.shape, BF16)] * 2
    return kernel_call(mask_kernel, "mask", outs, (sent, kept, sent_flags, kept_flags), 16, 1.3)


def head_masks():
    lane = lax.broadcasted_iota(jnp.int32, (1, PAIR), 1)
    low = (lane < PAIR // 2).astype(F32)
    return low, 1.0 - low


def masked(values, mask):
    return (values.astype(F32) * mask).astype(BF16)


def attention_kernel(q_ref, k_ref, v_ref, mixed_ref, level_ref):
    length, width = q_ref.shape
    ones = jnp.ones((length, PAIR), BF16)
    masks = head_masks()
    lane = lax.broadcasted_iota(jnp.int32, (1, PAIR), 1)
    levels = jnp.zeros((length, PAIR), F32)
    for pair in range(width // PAIR):
        cols = slice(pair * PAIR, (pair + 1) * PAIR)
        q, k, v = q_ref[:, cols], k_ref[:, cols], v_ref[:, cols]
        wide = jnp.concatenate([v, ones], axis=1)
        total = None
        for head, mask in enumerate(masks):
            scores = dot_nt(masked(q, mask), k)
            top = jnp.max(scores, axis=-1, keepdims=True)
            weights = jnp.exp(scores - top).astype(BF16)
            sums = dot(weights, wide)
            part = sums[:, :PAIR] * ((1.0 / sums[:, PAIR:]) * mask)
            total = part if total is None else total + part
            levels = jnp.where(lane == 2 * pair + head, top + jnp.log(sums[:, PAIR:]), levels)
        mixed_ref[:, cols] = total.astype(BF16)
    level_ref[...] = levels


def attention_call(q, k, v):
    length, width = q.shape
    outs = [shape((length, width), BF16), shape((length, PAIR), F32)]
    return kernel_call(
        attention_kernel, "attention", outs, (q, k, v), 16, 4.7
    )


def attention_back_kernel(begin, q_ref, k_ref, v_ref, mixed_ref, grad_ref, level_ref,
                          dq_ref, dk_ref, dv_ref):
    length, width = q_ref.shape
    masks = head_masks()
    half = PAIR // 2
    for pair in range(width // PAIR):
        cols = slice(pair * PAIR, (pair + 1) * PAIR)
        q, k, v = q_ref[:, cols], k_ref[:, cols], v_ref[:, cols]
        grad = grad_ref[begin : begin + length, cols]
        dots = grad.astype(F32) * mixed_ref[:, cols].astype(F32)
        grad_t = grad.T
        q_t = q.T
        dq = None
        dk, dv = [], []
        for head, mask in enumerate(masks):
            place = 2 * pair + head
            probs = jnp.exp(dot_nt(masked(q, mask), k) - level_ref[:, place : place + 1])
            grad_probs = dot_nt(masked(grad, mask), v)
            delta = jnp.sum(dots * mask, axis=-1, keepdims=True)
            scores = (probs * (grad_probs - delta)).astype(BF16)
            part = dot(scores, masked(k, mask))
            dq = part if dq is None else dq + part
            rows = slice(head * half, (head + 1) * half)
            dv.append(dot(grad_t, probs.astype(BF16))[rows])
            dk.append(dot(q_t, scores)[rows])
        dq_ref[:, cols] = (dq * 0.125).astype(BF16)
        dk_ref[:, cols] = jnp.concatenate(dk, axis=0).T.astype(BF16)
        dv_ref[:, cols] = jnp.concatenate(dv, axis=0).T.astype(BF16)


def attention_back_call(begin, q, k, v, mixed, grad, levels):
    length, width = q.shape
    outs = [shape((length, width), BF16)] * 3
    return kernel_call(
        functools.partial(attention_back_kernel, begin),
        "attention_back", outs, (q, k, v, mixed, grad, levels), 16, 7.8,
    )


def proj_kernel(mixed_one, mixed_two, own_one, own_two, other_one, other_two, w, b, gain, shift,
                resid_ref, second_ref):
    half = mixed_one.shape[0]
    rows_of = ((mixed_one, own_one, other_one), (mixed_two, own_two, other_two))
    for n, (mixed, own, other) in enumerate(rows_of):
        rows = slice(n * half, (n + 1) * half)
        resid = both(own, other).astype(F32) + (dot(mixed[...], w[...]) + b[...])
        resid_ref[rows, :] = resid
        unit, _ = normalize(resid)
        second_ref[rows, :] = (unit * gain[...] + shift[...]).astype(BF16)


def proj_call(*operands):
    half, width = operands[0].shape
    outs = [shape((2 * half, width), F32), shape((2 * half, width), BF16)]
    return kernel_call(proj_kernel, "proj", outs, operands, 16, 3.1)


def ffn_kernel(start, last, tiles, second_ref, grad_own, grad_other, w_in, b_in, w_out, b_out, base_ref, *refs):
    if start:
        out_ref, gs_ref, dw_ref, dbias_ref = refs
    else:
        more_ref, own_ref, other_ref, gs_ref, dw_ref, dbias_ref = refs
    tokens, width = second_ref.shape
    half = tokens // 4
    count = tokens // tiles
    for m in range(tiles):
        rows = slice(m * count, (m + 1) * count)
        second = second_ref[rows, :]
        pieces = [(n // 2, n % 2) for n in range(4)][m * 4 // tiles : (m + 1) * 4 // tiles]
        grad = jnp.concatenate(
            [(grad_other if side else grad_own)[n] for n, side in pieces], axis=0
        )
        out = base_ref[rows, :]
        gs = None if start else more_ref[rows, :]
        for n in range(w_in.shape[1] // width):
            cols = slice(n * width, (n + 1) * width)
            inner = dot(second, w_in[:, cols]) + b_in[:, cols]
            dact = dot_nt(grad, w_out[cols, :])
            phi = 0.5 * (1.0 + lax.erf(inner * ROOT_HALF))
            act = (inner * phi).astype(BF16)
            slope = phi + inner * jnp.exp(-0.5 * inner * inner) * ROOT_TWO_PI
            ginner = (dact * slope).astype(BF16)
            out = out + dot(act, w_out[cols, :])
            more = dot_nt(ginner, w_in[:, cols])
            gs = more if gs is None else gs + more
            d_out = dot_tn(act, grad)
            d_in = dot_tn(second, ginner)
            bias = column_sum(ginner)
            if m > 0:
                d_out = d_out + dw_ref[n, 1].astype(F32)
                d_in = d_in + dw_ref[n, 0].astype(F32)
                bias = bias + dbias_ref[:, cols]
            dw_ref[n, 1] = d_out.astype(BF16)
            dw_ref[n, 0] = d_in.astype(BF16)
            dbias_ref[:, cols] = bias
        gs_ref[rows, :] = gs
        if last:
            low = (out + b_out[...]).astype(BF16)
            for place, (row, side) in enumerate(pieces):
                (other_ref if side else own_ref)[row] = low[place * half : (place + 1) * half]
        else:
            out_ref[rows, :] = out


def ffn_call(start, last, number, *operands):
    tokens, width = operands[0].shape
    span = operands[3].shape[1] // 2
    pieces = [shape((2, tokens // 4, width), BF16)] * 2
    outs = (pieces if last else [shape((tokens, width), F32)]) + [
        shape((tokens, width), F32),
        shape((span // width, 2, width, width), BF16),
        shape((1, span), F32),
    ]
    once = pl.Buffered(1)
    cut = {
        3: pl.BlockSpec((width, span), lambda i: (0, number), pipeline_mode=once),
        4: pl.BlockSpec((1, span), lambda i: (0, number), pipeline_mode=once),
        5: pl.BlockSpec((span, width), lambda i: (number, 0), pipeline_mode=once),
    }
    return kernel_call(
        functools.partial(ffn_kernel, start, last, TILES),
        "ffn", outs, operands, FFN_LIMIT, 18.0, () if start else ((8, 2 if last else 1),),
        cut=cut,
    )


def proj_back_kernel(gs_ref, resid_ref, grad_own, grad_other, mixed_one, mixed_two, w, gain,
                     gresid_ref, gmixed_ref, dw_ref, vec_ref):
    unit, scale = normalize(resid_ref[...])
    gs = gs_ref[...]
    grad = four(grad_own, grad_other).astype(F32)
    gresid = grad + norm_back(gs, unit, scale, gain[...])
    gresid_ref[...] = gresid
    branch = gresid.astype(BF16)
    gmixed_ref[...] = dot_nt(branch, w[...]).astype(BF16)
    dw_ref[...] = dot_tn(both(mixed_one, mixed_two), branch).astype(BF16)
    sums = (column_sum(gs * unit), column_sum(gs), column_sum(branch), column_sum(grad))
    for n, total in enumerate(sums):
        vec_ref[n : n + 1, :] = total


def proj_back_call(*operands):
    tokens, width = operands[0].shape
    outs = [
        shape((tokens, width), F32),
        shape((tokens, width), BF16),
        shape((width, width), BF16),
        shape((4, width), F32),
    ]
    return kernel_call(
        proj_back_kernel, "proj_back", outs, operands, 24, 6.0, ((0, 0),)
    )


def qkv_weights_kernel(own_one, own_two, other_one, other_two, gain, shift, *refs):
    dw_ref, value_ref, vec_ref = refs[6:]
    firsts = []
    for own, other in ((own_one, other_one), (own_two, other_two)):
        unit, _ = normalize(both(own, other).astype(F32))
        firsts.append((unit * gain[...] + shift[...]).astype(BF16))
    first = jnp.concatenate(firsts, axis=0)
    for n in range(3):
        grad = both(refs[n], refs[3 + n])
        dw = dot_tn(first, grad).astype(BF16)
        if n < 2:
            dw_ref[n] = dw
        else:
            value_ref[...] = dw
        vec_ref[n : n + 1, :] = column_sum(grad)


def qkv_weights_call(*operands):
    length, width = operands[-1].shape
    outs = [shape((2, width, width), BF16), shape((width, width), BF16), shape((3, width), F32)]
    return kernel_call(qkv_weights_kernel, "qkv_weights", outs, operands, 20, 5.8)


VECTOR_ROWS = 64


def input_back_kernel(own_one, own_two, other_one, other_two, gresid_ref, wq, wk, wv, gain,
                      dw_value, dw_proj, vec_qkv, vec_two, bias_one, bias_two, *refs):
    own_ref, other_ref, rest_ref = refs[6:]
    half, width = own_one.shape
    totals = None
    for n, (own, other) in enumerate(((own_one, other_one), (own_two, other_two))):
        dq, dk, dv = refs[3 * n : 3 * n + 3]
        gfirst = dot_nt(dq[...], wq[...]) + dot_nt(dk[...], wk[...]) + dot_nt(dv[...], wv[...])
        unit, scale = normalize(both(own, other).astype(F32))
        rows = slice(2 * n * half, 2 * (n + 1) * half)
        gin = gresid_ref[rows, :] + norm_back(gfirst, unit, scale, gain[...])
        own_ref[n] = gin[:half].astype(BF16)
        other_ref[n] = gin[half:].astype(BF16)
        sums = (column_sum(gfirst * unit), column_sum(gfirst))
        totals = sums if totals is None else tuple(a + b for a, b in zip(totals, sums))
    vectors = list(totals) + [vec_two[n : n + 1, :] for n in range(4)]
    vectors += [vec_qkv[0:1, :], vec_qkv[2:3, :]]
    for bias in (bias_one, bias_two):
        for n in range(bias.shape[1] // width):
            vectors.append(bias[:, n * width : (n + 1) * width])
    vectors.append(jnp.zeros((VECTOR_ROWS - len(vectors), width), F32))
    rest_ref[0, :width, :] = dw_value[...]
    rest_ref[0, width:, :] = jnp.concatenate(vectors, axis=0).astype(BF16)
    rest_ref[1, :width, :] = dw_proj[...]
    rest_ref[1, width:, :] = jnp.zeros((VECTOR_ROWS, width), BF16)


def input_back_call(*operands):
    half, width = operands[0].shape
    outs = [shape((2, half, width), BF16)] * 2 + [shape((2, width + VECTOR_ROWS, width), BF16)]
    return kernel_call(input_back_kernel, "input_back", outs, operands, 20, 7.0)


CHUNKS = 4


def place_call(sides, job, skip, hidden, earlier, core_number):
    chain = CHAIN[-1]
    operands = job.result
    width = operands[0].shape[1]
    rows = width // CHUNKS

    def body(sides_ref, mine_ref, other_ref, *refs):
        inner_ref, outer_ref, token_ref = refs[-3:]
        block, chunk = pl.program_id(0), pl.program_id(1)
        first = pl.ds(pl.multiple_of(chunk * rows, 16), rows)
        second = pl.ds(pl.multiple_of(width + chunk * rows, 16), rows)
        for ref, wanted in ((mine_ref, True), (other_ref, False)):

            @pl.when((sides_ref[core_number] == block) == wanted)
            def _():
                inner_ref[...] = ref[first, :].astype(F32)
                outer_ref[...] = ref[second, :].astype(F32)

        token_ref[...] = jnp.zeros((8, PAIR), F32)

    results = pl.pallas_call(
        body,
        grid=(2, CHUNKS),
        in_specs=[pl.BlockSpec(memory_space=pltpu.SMEM)]
        + [VM] * 3
        + [pl.BlockSpec(memory_space=pl.ANY)] * len(earlier),
        out_specs=[
            pl.BlockSpec((rows, width), lambda j, c: (c, j + skip)),
            pl.BlockSpec((rows, width), lambda j, c: ((j + skip) * CHUNKS + c, 0)),
            VM,
        ],
        out_shape=[
            shape((width, hidden), F32), shape((hidden, width), F32), shape((8, PAIR), F32),
        ],
        input_output_aliases={4 + n: n for n in range(len(earlier))},
        compiler_params=pltpu.CompilerParams(vmem_limit_bytes=8 * MIB),
        cost_estimate=cost_of(5.0),
        name="place",
    )(sides, *operands, chain.token, *earlier)
    chain.token = results[-1]
    return results[:-1]


def spread_call(sides, job, core_number):
    chain = CHAIN[-1]
    operands = job.result
    total, width = operands[0].shape
    rows = width // CHUNKS
    more = total - width

    def body(sides_ref, mine_ref, other_ref, token_in, low_ref, high_ref, *refs):
        here = pl.ds(pl.multiple_of(pl.program_id(0) * rows, 16), rows)
        for side in range(2):
            low, high = (mine_ref, other_ref) if side == 0 else (other_ref, mine_ref)

            @pl.when(sides_ref[core_number] == side)
            def _():
                low_ref[...] = low[here, :].astype(F32)
                high_ref[...] = high[here, :].astype(F32)
                if more:
                    refs[0][...] = low[width:, :].astype(F32)

        refs[-1][...] = jnp.zeros((8, PAIR), F32)

    part = pl.BlockSpec((rows, width), lambda c: (c, 0))
    results = pl.pallas_call(
        body,
        grid=(CHUNKS,),
        in_specs=[pl.BlockSpec(memory_space=pltpu.SMEM)] + [VM] * 3,
        out_specs=[part, part] + [VM] * (2 if more else 1),
        out_shape=[shape((width, width), F32)] * 2
        + ([shape((more, width), F32)] if more else [])
        + [shape((8, PAIR), F32)],
        compiler_params=pltpu.CompilerParams(vmem_limit_bytes=8 * MIB),
        cost_estimate=cost_of(3.0),
        name="spread",
    )(sides, *operands, chain.token)
    chain.token = results[-1]
    return results[:-1]


AXES = ("blk", "far", "x", "core")
BIT_OF = {"x": ("x", 0), "y": ("blk", 0), "z": ("far", 0), "w": ("far", 1)}


class Hop:
    def __init__(self, number, sizes, steps):
        self.number, self.sizes, self.steps = number, sizes, steps

    def swap(self, values):
        dims = [self.sizes[axis] for axis in AXES]
        pairs = []
        for device in range(math.prod(dims)):
            place, left = [], device
            for size in reversed(dims):
                place.insert(0, left % size)
                left //= size
            axis, bit = self.steps[place[-1]]
            place[AXES.index(axis)] ^= 1 << bit
            target = 0
            for size, coordinate in zip(dims, place):
                target = target * size + coordinate
            pairs.append((device, target))
        return lax.ppermute(values, AXES, pairs)

    def side(self):
        first, second = ((lax.axis_index(axis) >> bit) % 2 for axis, bit in self.steps)
        return jnp.where(lax.axis_index("core") == 0, first, second)


class Hops:
    def __init__(self, sizes):
        self.sizes, self.known = sizes, {}
        self.deep = [("far", bit) for bit in range(2, sizes["far"].bit_length() - 1)]

    def of(self, steps):
        if steps not in self.known:
            self.known[steps] = Hop(len(self.known), self.sizes, steps)
        return self.known[steps]

    def named(self, names):
        found = []
        for name in filter(None, names.split(".")):
            steps = ("core", 0) if name == "c" else None
            pair = (steps, steps) if steps else tuple(BIT_OF[letter] for letter in name)
            found.append(self.of(pair))
        return found

    def rest(self):
        return [self.of((step, step)) for step in self.deep]

    def sides(self):
        return jnp.stack([hop.side() for hop in self.known.values()]).astype(jnp.int32)


class Job:
    def __init__(self, steps):
        self.steps, self.waiting, self.result = steps, None, None
        self.advance()

    def advance(self):
        try:
            hop, values = self.steps.send(self.waiting)
        except StopIteration as stop:
            self.result, self.waiting = stop.value, None
            return
        self.waiting = hop.swap(values)

    def done(self):
        return self.waiting is None


class Part:
    def __init__(self, values, cuts=()):
        self.values, self.cuts = values, cuts

    def cut(self, hop, rows):
        return Part(self.values, self.cuts + ((hop.number, rows),))


def begin_of(sides_ref, cuts, flipped=None):
    total = 0
    for number, rows in cuts:
        total = total + sides_ref[number] * rows
    if flipped is not None:
        number, rows = flipped
        total = total + (1 - sides_ref[number]) * rows
    return total


def add_cost(rows):
    return 0.7 + ADD_SLOPE * rows / 768


def add_call(sides, parts, rows, flipped=None):
    width = parts[0].values.shape[1]
    assert rows % 16 == 0

    def body(sides_ref, *refs):
        total = None
        for ref, part in zip(refs, parts):
            begin = begin_of(sides_ref, part.cuts, flipped)
            if not isinstance(begin, int):
                begin = pl.multiple_of(begin, 16)
            piece = ref[pl.ds(begin, rows), :].astype(F32)
            total = piece if total is None else total + piece
        refs[-1][...] = total.astype(BF16)

    operands = (sides,) + tuple(part.values for part in parts)
    return kernel_call(
        body, "add", [shape((rows, width), BF16)], operands, 16, add_cost(rows), scalars=1
    )[0]


def join_call(sides, hop, mine, other):
    rows, width = mine.shape
    assert rows % 16 == 0

    def body(sides_ref, mine_ref, other_ref, out_ref):
        side = sides_ref[hop.number]
        out_ref[pl.ds(pl.multiple_of(side * rows, 16), rows), :] = mine_ref[...]
        out_ref[pl.ds(pl.multiple_of((1 - side) * rows, 16), rows), :] = other_ref[...]

    outs = [shape((2 * rows, width), BF16)]
    return kernel_call(body, "join", outs, (sides, mine, other), 16, 0.9, scalars=1)[0]


def sum_steps(sides, values, scatter, exchange):
    rows = values.shape[0]
    parts = [Part(values)]
    for hop in scatter:
        rows //= 2
        sent = add_call(sides, parts, rows, (hop.number, rows))
        got = yield hop, sent
        parts = [part.cut(hop, rows) for part in parts] + [Part(got)]
    for hop in exchange:
        whole = add_call(sides, parts, rows)
        got = yield hop, whole
        parts = [Part(whole), Part(got)]
    whole = add_call(sides, parts, rows)
    for hop in reversed(scatter[1:]):
        other = yield hop, whole
        whole = join_call(sides, hop, whole, other)
    other = yield scatter[0], whole
    return whole, other


PLAN = {
    "F0": ("c.xy.wx", "zw.yz"),
    "F1": ("c.zx.xy.yw", "wz"),
    "qk": ("c.yx.xz.zw.wy", ""),
    "rest": ("c.xz.wy", "zx.yw"),
}
SCHEDULE = (
    "ffn0", "F0", "F0", "ffn1", "F1", "out", "F0", "F1",
    "proj_back", "ab0", "F0", "F1", "ab1", "F1", "out", "F0",
    "qw", "qk", "F0", "F1", "qk", "ib", "gin", "rest",
    "qk", "F1", "rest", "qk", "F0", "qk", "F1", "rest",
    "qk", "gin", "qk", "rest", "qk", "F1", "rest", "F0",
    "qk", "rest", "F0", "rest", "qk", "F1", "qk", "rest",
    "F1", "rest",
)


def home_call(sides, hop, kept, back):
    rows = kept.shape[0]

    def body(sides_ref, kept_ref, back_ref, out_ref):
        side = sides_ref[hop.number]
        out_ref[pl.ds(side * rows, rows)] = kept_ref[...]
        out_ref[pl.ds((1 - side) * rows, rows)] = back_ref[...]

    outs = [shape((2 * rows,) + kept.shape[1:], BF16)]
    return kernel_call(body, "home", outs, (sides, kept, back), 16, 1.0, scalars=1)[0]


def home_steps(sides, hop, kept, values):
    back = yield hop, values
    return home_call(sides, hop, kept, back)


def swap_steps(hop, values):
    got = yield hop, values
    return got


def on_device(
    sizes,
    inputs,
    cotangent,
    flags,
    gain_one,
    shift_one,
    query_weight,
    query_bias,
    key_weight,
    value_weight,
    value_bias,
    proj_weight,
    proj_bias,
    gain_two,
    shift_two,
    inner_weight,
    inner_bias,
    outer_weight,
    outer_bias,
):
    batch, half, width = inputs.shape
    hidden = inner_weight.shape[1]
    rows = batch // 2
    assert rows == 2 and sizes["blk"] == 2
    length = 2 * half

    hops = Hops(sizes)
    y_hop = hops.named("yy")[0]
    planned = {
        name: (hops.named(scatter), hops.named(exchange) + hops.rest())
        for name, (scatter, exchange) in PLAN.items()
    }
    sides = hops.sides()

    def row(vector):
        return vector.reshape(1, -1)

    CHAIN.append(Chain())

    blk = lax.axis_index("blk")

    def kept_rows(values):
        return lax.dynamic_slice_in_dim(values, blk * rows, rows, 0)

    def sent_rows(values):
        return lax.dynamic_slice_in_dim(values, (1 - blk) * rows, rows, 0)

    def strides(values):
        return values.reshape(rows, half, -1)

    sent = sent_rows(inputs)
    arriving = [Job(swap_steps(y_hop, sent[n])) for n in range(rows)]
    kept = kept_rows(inputs)
    owns = [kept[n] for n in range(rows)]

    weights_one = (
        row(gain_one), row(shift_one), query_weight, key_weight, value_weight,
        row(query_bias), row(value_bias),
    )
    others, qs, ks, vs, mixes, levels = [], [], [], [], [], []
    for n in range(rows):
        arriving[n].advance()
        others.append(arriving[n].result)
        q, k, v = qkv_call(owns[n], others[n], *weights_one)
        if n == rows - 1:
            grad_job = Job(swap_steps(y_hop, grad_sent))
        mixed, level = attention_call(q, k, v)
        if n == 0:
            grad_sent, grad_own = mask_call(
                sent_rows(cotangent), kept_rows(cotangent),
                strides(sent_rows(flags)), strides(kept_rows(flags)),
            )
        for kind, values in zip((qs, ks, vs, mixes, levels), (q, k, v, mixed, level)):
            kind.append(values)
    resid, second = proj_call(
        *mixes, *owns, *others, proj_weight, row(proj_bias), row(gain_two), row(shift_two)
    )
    grad_job.advance()
    grads_out = (grad_own, grad_job.result)

    middle = hidden // 2

    weights_two = (inner_weight, row(inner_bias), outer_weight, row(outer_bias))

    made = {}

    def ffn0():
        return ffn_call(True, False, 0, second, *grads_out, *weights_two, resid)

    def ffn1():
        out, gs = made["ffn0"][:2]
        return ffn_call(False, True, 1, second, *grads_out, *weights_two, out, gs)

    def proj_back():
        return proj_back_call(
            made["ffn1"][2], resid, *grads_out, *mixes, proj_weight, row(gain_two)
        )

    def attention_back(n):
        return attention_back_call(
            n * length, qs[n], ks[n], vs[n], mixes[n], made["proj_back"][1], levels[n]
        )

    def qkv_weights():
        return qkv_weights_call(
            *owns, *others, row(gain_one), row(shift_one), *made["ab0"], *made["ab1"]
        )

    def input_back():
        return input_back_call(
            *owns, *others, made["proj_back"][0], query_weight, key_weight, value_weight,
            row(gain_one), made["qw"][1], made["proj_back"][2], made["qw"][2],
            made["proj_back"][3], made["ffn0"][3], made["ffn1"][4], *made["ab0"], *made["ab1"],
        )

    kernels = {
        "ffn0": ffn0,
        "ffn1": ffn1,
        "proj_back": proj_back,
        "ab0": lambda: attention_back(0),
        "ab1": lambda: attention_back(1),
        "qw": qkv_weights,
        "ib": input_back,
    }
    starts = {
        "F0": lambda: made["ffn0"][2],
        "F1": lambda: made["ffn1"][3],
        "qk": lambda: made["qw"][0],
        "rest": lambda: made["ib"][2],
    }
    homes = {
        "out": lambda: made["ffn1"][:2],
        "gin": lambda: made["ib"][:2],
    }
    jobs, places = {}, ()

    def step(name):
        nonlocal places
        if name in kernels:
            made[name] = kernels[name]()
        elif name not in jobs:
            if name in homes:
                jobs[name] = Job(home_steps(sides, y_hop, *homes[name]()))
            else:
                values = starts[name]().reshape(-1, width)
                jobs[name] = Job(sum_steps(sides, values, *planned[name]))
        elif not jobs[name].done():
            jobs[name].advance()
            if not jobs[name].done() or name in homes:
                return
            core_number = planned[name][0][0].number
            if name in ("F0", "F1"):
                skip = 0 if name == "F0" else middle // width
                places = place_call(sides, jobs[name], skip, hidden, places, core_number)
            else:
                made[name] = spread_call(sides, jobs[name], core_number)

    for name in SCHEDULE:
        step(name)
    while not all(job.done() for job in jobs.values()):
        for name in jobs:
            step(name)
    CHAIN.pop()
    inner_weight_grad, outer_weight_grad = places
    query_grad, key_grad = made["qk"]
    value_grad, proj_grad, totals = made["rest"]
    return (
        jobs["out"].result,
        jobs["gin"].result,
        totals[0],
        totals[1],
        query_grad,
        totals[6],
        key_grad,
        value_grad,
        totals[7],
        proj_grad,
        totals[4],
        totals[2],
        totals[3],
        inner_weight_grad,
        totals[8 : 8 + hidden // width].reshape(-1),
        outer_weight_grad,
        totals[5],
    )


def solution(mesh):
    sizes = dict(mesh.shape)
    far = sizes["dp"] // 4
    fine = Mesh(mesh.devices.reshape(sizes["blk"], far, 2, 2), ("blk", "far", "x", "core"))
    rows = ("far", "x", "core")
    split = P(rows, "blk", None)
    in_specs = (split, split, P(rows, "blk")) + (P(),) * 15
    out_specs = (split, split) + (P(),) * 15
    return jax.shard_map(
        functools.partial(on_device, dict(fine.shape)),
        mesh=fine,
        in_specs=in_specs,
        out_specs=out_specs,
        check_vma=False,
    )
```

```python
import functools
import math

import jax
import jax.numpy as jnp
from jax import lax
from jax.experimental import pallas as pl
from jax.experimental.pallas import tpu as pltpu
from jax.sharding import Mesh, PartitionSpec as P

EPS = 1e-05
F32 = jnp.float32
BF16 = jnp.bfloat16
PAIR = 128
MIB = 1024 * 1024
ROOT_HALF = 0.7071067811865476
ROOT_TWO_PI = 0.3989422804014327
VM = pl.BlockSpec(memory_space=pltpu.VMEM)
TILES = 2
FFN_LIMIT = 15


def dot(left, right):
    return lax.dot_general(left, right, (((1,), (0,)), ((), ())), preferred_element_type=F32)


def dot_nt(left, right):
    return lax.dot_general(left, right, (((1,), (1,)), ((), ())), preferred_element_type=F32)


def dot_tn(left, right):
    return lax.dot_general(left, right, (((0,), (0,)), ((), ())), preferred_element_type=F32)


def normalize(values):
    center = values - jnp.mean(values, axis=-1, keepdims=True)
    scale = lax.rsqrt(jnp.mean(center * center, axis=-1, keepdims=True) + EPS)
    return center * scale, scale


def norm_back(grad, unit, scale, gain):
    scaled = grad * gain
    return scale * (
        scaled
        - jnp.mean(scaled, axis=-1, keepdims=True)
        - unit * jnp.mean(scaled * unit, axis=-1, keepdims=True)
    )


def both(one_ref, two_ref):
    return jnp.concatenate([one_ref[...], two_ref[...]], axis=0)


def four(own_ref, other_ref):
    return jnp.concatenate([own_ref[0], other_ref[0], own_ref[1], other_ref[1]], axis=0)


def column_sum(values):
    return jnp.sum(values.astype(F32), axis=0, keepdims=True)


def shape(dims, dtype):
    return jax.ShapeDtypeStruct(dims, dtype)


class Chain:
    def __init__(self):
        self.token = jnp.zeros((8, PAIR), F32)


CHAIN = []
SHARE = 10.0
ADD_SLOPE = 1.2
BYTES = 200.0


def cost_of(us):
    flops, size = int(us * SHARE * 1.15e9), int(us * BYTES * 3.3e6)
    return pl.CostEstimate(flops=flops, bytes_accessed=size, transcendentals=0)


def kernel_call(body, name, outs, operands, limit, us, aliases=(), scalars=0, cut=None):
    chain = CHAIN[-1]
    count = len(operands)

    def whole(*refs):
        body(*refs[:count], *refs[count + 1 : -1])
        refs[-1][...] = jnp.zeros((8, PAIR), F32)

    specs = [pl.BlockSpec(memory_space=pltpu.SMEM)] * scalars + [VM] * (count + 1 - scalars)
    for place, spec in (cut or {}).items():
        specs[place] = spec
    results = pl.pallas_call(
        whole,
        grid=(1,) if cut else (),
        in_specs=specs,
        out_specs=[VM] * (len(outs) + 1),
        out_shape=list(outs) + [shape((8, PAIR), F32)],
        input_output_aliases=dict(aliases),
        compiler_params=pltpu.CompilerParams(vmem_limit_bytes=limit * MIB),
        cost_estimate=cost_of(us),
        name=name,
    )(*operands, chain.token)
    chain.token = results[-1]
    return results[:-1]


def qkv_kernel(own_ref, other_ref, gain, shift, wq, wk, wv, bq, bv, q_ref, k_ref, v_ref):
    unit, _ = normalize(both(own_ref, other_ref).astype(F32))
    first = (unit * gain[...] + shift[...]).astype(BF16)
    q_ref[...] = ((dot(first, wq[...]) + bq[...]).astype(BF16).astype(F32) * 0.125).astype(BF16)
    k_ref[...] = dot(first, wk[...]).astype(BF16)
    v_ref[...] = (dot(first, wv[...]) + bv[...]).astype(BF16)


def qkv_call(own, other, *weights):
    half, width = own.shape
    outs = [shape((2 * half, width), BF16)] * 3
    return kernel_call(
        qkv_kernel, "qkv", outs, (own, other) + weights, 16, 3.0
    )


def mask_kernel(sent_ref, kept_ref, sent_flags, kept_flags, sent_out, kept_out):
    for values, flags, out in ((sent_ref, sent_flags, sent_out), (kept_ref, kept_flags, kept_out)):
        keep = jnp.max(flags[...], axis=-1, keepdims=True)
        out[...] = (values[...].astype(F32) * keep.astype(F32)).astype(BF16)


def mask_call(sent, kept, sent_flags, kept_flags):
    outs = [shape(sent.shape, BF16)] * 2
    return kernel_call(mask_kernel, "mask", outs, (sent, kept, sent_flags, kept_flags), 16, 1.3)


def head_masks():
    lane = lax.broadcasted_iota(jnp.int32, (1, PAIR), 1)
    low = (lane < PAIR // 2).astype(F32)
    return low, 1.0 - low


def masked(values, mask):
    return (values.astype(F32) * mask).astype(BF16)


def attention_kernel(q_ref, k_ref, v_ref, mixed_ref, level_ref):
    length, width = q_ref.shape
    ones = jnp.ones((length, PAIR), BF16)
    masks = head_masks()
    lane = lax.broadcasted_iota(jnp.int32, (1, PAIR), 1)
    levels = jnp.zeros((length, PAIR), F32)
    for pair in range(width // PAIR):
        cols = slice(pair * PAIR, (pair + 1) * PAIR)
        q, k, v = q_ref[:, cols], k_ref[:, cols], v_ref[:, cols]
        wide = jnp.concatenate([v, ones], axis=1)
        total = None
        for head, mask in enumerate(masks):
            scores = dot_nt(masked(q, mask), k)
            top = jnp.max(scores, axis=-1, keepdims=True)
            weights = jnp.exp(scores - top).astype(BF16)
            sums = dot(weights, wide)
            part = sums[:, :PAIR] * ((1.0 / sums[:, PAIR:]) * mask)
            total = part if total is None else total + part
            levels = jnp.where(lane == 2 * pair + head, top + jnp.log(sums[:, PAIR:]), levels)
        mixed_ref[:, cols] = total.astype(BF16)
    level_ref[...] = levels


def attention_call(q, k, v):
    length, width = q.shape
    outs = [shape((length, width), BF16), shape((length, PAIR), F32)]
    return kernel_call(
        attention_kernel, "attention", outs, (q, k, v), 16, 4.7
    )


def attention_back_kernel(begin, q_ref, k_ref, v_ref, mixed_ref, grad_ref, level_ref,
                          dq_ref, dk_ref, dv_ref):
    length, width = q_ref.shape
    masks = head_masks()
    half = PAIR // 2
    for pair in range(width // PAIR):
        cols = slice(pair * PAIR, (pair + 1) * PAIR)
        q, k, v = q_ref[:, cols], k_ref[:, cols], v_ref[:, cols]
        grad = grad_ref[begin : begin + length, cols]
        dots = grad.astype(F32) * mixed_ref[:, cols].astype(F32)
        grad_t = grad.T
        q_t = q.T
        dq = None
        dk, dv = [], []
        for head, mask in enumerate(masks):
            place = 2 * pair + head
            probs = jnp.exp(dot_nt(masked(q, mask), k) - level_ref[:, place : place + 1])
            grad_probs = dot_nt(masked(grad, mask), v)
            delta = jnp.sum(dots * mask, axis=-1, keepdims=True)
            scores = (probs * (grad_probs - delta)).astype(BF16)
            part = dot(scores, masked(k, mask))
            dq = part if dq is None else dq + part
            rows = slice(head * half, (head + 1) * half)
            dv.append(dot(grad_t, probs.astype(BF16))[rows])
            dk.append(dot(q_t, scores)[rows])
        dq_ref[:, cols] = (dq * 0.125).astype(BF16)
        dk_ref[:, cols] = jnp.concatenate(dk, axis=0).T.astype(BF16)
        dv_ref[:, cols] = jnp.concatenate(dv, axis=0).T.astype(BF16)


def attention_back_call(begin, q, k, v, mixed, grad, levels):
    length, width = q.shape
    outs = [shape((length, width), BF16)] * 3
    return kernel_call(
        functools.partial(attention_back_kernel, begin),
        "attention_back", outs, (q, k, v, mixed, grad, levels), 16, 7.8,
    )


def proj_kernel(mixed_one, mixed_two, own_one, own_two, other_one, other_two, w, b, gain, shift,
                resid_ref, second_ref):
    half = mixed_one.shape[0]
    rows_of = ((mixed_one, own_one, other_one), (mixed_two, own_two, other_two))
    for n, (mixed, own, other) in enumerate(rows_of):
        rows = slice(n * half, (n + 1) * half)
        resid = both(own, other).astype(F32) + (dot(mixed[...], w[...]) + b[...])
        resid_ref[rows, :] = resid
        unit, _ = normalize(resid)
        second_ref[rows, :] = (unit * gain[...] + shift[...]).astype(BF16)


def proj_call(*operands):
    half, width = operands[0].shape
    outs = [shape((2 * half, width), F32), shape((2 * half, width), BF16)]
    return kernel_call(proj_kernel, "proj", outs, operands, 16, 3.1)


def ffn_kernel(start, last, tiles, second_ref, grad_own, grad_other, w_in, b_in, w_out, b_out, base_ref, *refs):
    if start:
        out_ref, gs_ref, dw_ref, dbias_ref = refs
    else:
        more_ref, own_ref, other_ref, gs_ref, dw_ref, dbias_ref = refs
    tokens, width = second_ref.shape
    half = tokens // 4
    count = tokens // tiles
    for m in range(tiles):
        rows = slice(m * count, (m + 1) * count)
        second = second_ref[rows, :]
        pieces = [(n // 2, n % 2) for n in range(4)][m * 4 // tiles : (m + 1) * 4 // tiles]
        grad = jnp.concatenate(
            [(grad_other if side else grad_own)[n] for n, side in pieces], axis=0
        )
        out = base_ref[rows, :]
        gs = None if start else more_ref[rows, :]
        for n in range(w_in.shape[1] // width):
            cols = slice(n * width, (n + 1) * width)
            inner = dot(second, w_in[:, cols]) + b_in[:, cols]
            dact = dot_nt(grad, w_out[cols, :])
            phi = 0.5 * (1.0 + lax.erf(inner * ROOT_HALF))
            act = (inner * phi).astype(BF16)
            slope = phi + inner * jnp.exp(-0.5 * inner * inner) * ROOT_TWO_PI
            ginner = (dact * slope).astype(BF16)
            out = out + dot(act, w_out[cols, :])
            more = dot_nt(ginner, w_in[:, cols])
            gs = more if gs is None else gs + more
            d_out = dot_tn(act, grad)
            d_in = dot_tn(second, ginner)
            bias = column_sum(ginner)
            if m > 0:
                d_out = d_out + dw_ref[n, 1].astype(F32)
                d_in = d_in + dw_ref[n, 0].astype(F32)
                bias = bias + dbias_ref[:, cols]
            dw_ref[n, 1] = d_out.astype(BF16)
            dw_ref[n, 0] = d_in.astype(BF16)
            dbias_ref[:, cols] = bias
        gs_ref[rows, :] = gs
        if last:
            low = (out + b_out[...]).astype(BF16)
            for place, (row, side) in enumerate(pieces):
                (other_ref if side else own_ref)[row] = low[place * half : (place + 1) * half]
        else:
            out_ref[rows, :] = out


def ffn_call(start, last, number, *operands):
    tokens, width = operands[0].shape
    span = operands[3].shape[1] // 2
    pieces = [shape((2, tokens // 4, width), BF16)] * 2
    outs = (pieces if last else [shape((tokens, width), F32)]) + [
        shape((tokens, width), F32),
        shape((span // width, 2, width, width), BF16),
        shape((1, span), F32),
    ]
    once = pl.Buffered(1)
    cut = {
        3: pl.BlockSpec((width, span), lambda i: (0, number), pipeline_mode=once),
        4: pl.BlockSpec((1, span), lambda i: (0, number), pipeline_mode=once),
        5: pl.BlockSpec((span, width), lambda i: (number, 0), pipeline_mode=once),
    }
    return kernel_call(
        functools.partial(ffn_kernel, start, last, TILES),
        "ffn", outs, operands, FFN_LIMIT, 18.0, () if start else ((8, 2 if last else 1),),
        cut=cut,
    )


def proj_back_kernel(gs_ref, resid_ref, grad_own, grad_other, mixed_one, mixed_two, w, gain,
                     gresid_ref, gmixed_ref, dw_ref, vec_ref):
    unit, scale = normalize(resid_ref[...])
    gs = gs_ref[...]
    grad = four(grad_own, grad_other).astype(F32)
    gresid = grad + norm_back(gs, unit, scale, gain[...])
    gresid_ref[...] = gresid
    branch = gresid.astype(BF16)
    gmixed_ref[...] = dot_nt(branch, w[...]).astype(BF16)
    dw_ref[...] = dot_tn(both(mixed_one, mixed_two), branch).astype(BF16)
    sums = (column_sum(gs * unit), column_sum(gs), column_sum(branch), column_sum(grad))
    for n, total in enumerate(sums):
        vec_ref[n : n + 1, :] = total


def proj_back_call(*operands):
    tokens, width = operands[0].shape
    outs = [
        shape((tokens, width), F32),
        shape((tokens, width), BF16),
        shape((width, width), BF16),
        shape((4, width), F32),
    ]
    return kernel_call(
        proj_back_kernel, "proj_back", outs, operands, 24, 6.0, ((0, 0),)
    )


VECTOR_ROWS = 64


def qkv_weights_kernel(own_one, own_two, other_one, other_two, gain, shift, wq, wk, wv,
                       dw_proj, vec_two, bias_one, bias_two, *refs):
    dw_ref, rest_ref = refs[6:]
    width = own_one.shape[1]
    units = [
        normalize(both(own, other).astype(F32))[0].astype(BF16)
        for own, other in ((own_one, other_one), (own_two, other_two))
    ]
    unit = jnp.concatenate(units, axis=0)
    gains, shifts = gain[...], shift[...]
    sums, by_gain, by_shift = [], None, None
    for n, w in enumerate((wq, wk, wv)):
        grad = both(refs[n], refs[3 + n])
        terms = dot_tn(unit, grad)
        total = column_sum(grad)
        weight = w[...].astype(F32)
        dw = (terms * gains + shifts * total).astype(BF16)
        if n < 2:
            dw_ref[n] = dw
        else:
            rest_ref[0, :width, :] = dw
        gained, shifted = weight * terms, weight * total
        by_gain = gained if by_gain is None else by_gain + gained
        by_shift = shifted if by_shift is None else by_shift + shifted
        sums.append(total)
    lane = lax.broadcasted_iota(jnp.int32, (1, PAIR), 1)
    columns = jnp.where(
        lane == 0,
        jnp.sum(by_gain, axis=-1, keepdims=True),
        jnp.sum(by_shift, axis=-1, keepdims=True),
    )
    vectors = [columns.T[:2], vec_two[...], sums[0], sums[2]]
    for bias in (bias_one, bias_two):
        for n in range(bias.shape[1] // width):
            vectors.append(bias[:, n * width : (n + 1) * width])
    count = sum(part.shape[0] for part in vectors)
    vectors.append(jnp.zeros((VECTOR_ROWS - count, width), F32))
    rest_ref[0, width:, :] = jnp.concatenate(vectors, axis=0).astype(BF16)
    rest_ref[1, :width, :] = dw_proj[...]
    rest_ref[1, width:, :] = jnp.zeros((VECTOR_ROWS, width), BF16)


def qkv_weights_call(*operands):
    length, width = operands[-1].shape
    outs = [
        shape((2, width, width), BF16), shape((2, width + VECTOR_ROWS, width), BF16),
    ]
    return kernel_call(qkv_weights_kernel, "qkv_weights", outs, operands, 24, 6.5)


def input_back_kernel(own_one, own_two, other_one, other_two, gresid_ref, wq, wk, wv, gain, *refs):
    own_ref, other_ref = refs[6:]
    half = own_one.shape[0]
    for n, (own, other) in enumerate(((own_one, other_one), (own_two, other_two))):
        dq, dk, dv = refs[3 * n : 3 * n + 3]
        gfirst = dot_nt(dq[...], wq[...]) + dot_nt(dk[...], wk[...]) + dot_nt(dv[...], wv[...])
        unit, scale = normalize(both(own, other).astype(F32))
        rows = slice(2 * n * half, 2 * (n + 1) * half)
        gin = gresid_ref[rows, :] + norm_back(gfirst, unit, scale, gain[...])
        own_ref[n] = gin[:half].astype(BF16)
        other_ref[n] = gin[half:].astype(BF16)


def input_back_call(*operands):
    half, width = operands[0].shape
    outs = [shape((2, half, width), BF16)] * 2
    return kernel_call(input_back_kernel, "input_back", outs, operands, 16, 6.2)


CHUNKS = 4


def place_call(sides, job, skip, hidden, earlier, core_number):
    chain = CHAIN[-1]
    operands = job.result
    width = operands[0].shape[1]
    rows = width // CHUNKS

    def body(sides_ref, mine_ref, other_ref, *refs):
        inner_ref, outer_ref, token_ref = refs[-3:]
        block, chunk = pl.program_id(0), pl.program_id(1)
        first = pl.ds(pl.multiple_of(chunk * rows, 16), rows)
        second = pl.ds(pl.multiple_of(width + chunk * rows, 16), rows)
        for ref, wanted in ((mine_ref, True), (other_ref, False)):

            @pl.when((sides_ref[core_number] == block) == wanted)
            def _():
                inner_ref[...] = ref[first, :].astype(F32)
                outer_ref[...] = ref[second, :].astype(F32)

        token_ref[...] = jnp.zeros((8, PAIR), F32)

    results = pl.pallas_call(
        body,
        grid=(2, CHUNKS),
        in_specs=[pl.BlockSpec(memory_space=pltpu.SMEM)]
        + [VM] * 3
        + [pl.BlockSpec(memory_space=pl.ANY)] * len(earlier),
        out_specs=[
            pl.BlockSpec((rows, width), lambda j, c: (c, j + skip)),
            pl.BlockSpec((rows, width), lambda j, c: ((j + skip) * CHUNKS + c, 0)),
            VM,
        ],
        out_shape=[
            shape((width, hidden), F32), shape((hidden, width), F32), shape((8, PAIR), F32),
        ],
        input_output_aliases={4 + n: n for n in range(len(earlier))},
        compiler_params=pltpu.CompilerParams(vmem_limit_bytes=8 * MIB),
        cost_estimate=cost_of(5.0),
        name="place",
    )(sides, *operands, chain.token, *earlier)
    chain.token = results[-1]
    return results[:-1]


def spread_call(sides, job, core_number):
    chain = CHAIN[-1]
    operands = job.result
    total, width = operands[0].shape
    rows = width // CHUNKS
    more = total - width

    def body(sides_ref, mine_ref, other_ref, token_in, low_ref, high_ref, *refs):
        here = pl.ds(pl.multiple_of(pl.program_id(0) * rows, 16), rows)
        for side in range(2):
            low, high = (mine_ref, other_ref) if side == 0 else (other_ref, mine_ref)

            @pl.when(sides_ref[core_number] == side)
            def _():
                low_ref[...] = low[here, :].astype(F32)
                high_ref[...] = high[here, :].astype(F32)
                if more:
                    refs[0][...] = low[width:, :].astype(F32)

        refs[-1][...] = jnp.zeros((8, PAIR), F32)

    part = pl.BlockSpec((rows, width), lambda c: (c, 0))
    results = pl.pallas_call(
        body,
        grid=(CHUNKS,),
        in_specs=[pl.BlockSpec(memory_space=pltpu.SMEM)] + [VM] * 3,
        out_specs=[part, part] + [VM] * (2 if more else 1),
        out_shape=[shape((width, width), F32)] * 2
        + ([shape((more, width), F32)] if more else [])
        + [shape((8, PAIR), F32)],
        compiler_params=pltpu.CompilerParams(vmem_limit_bytes=8 * MIB),
        cost_estimate=cost_of(3.0),
        name="spread",
    )(sides, *operands, chain.token)
    chain.token = results[-1]
    return results[:-1]


AXES = ("blk", "far", "x", "core")
BIT_OF = {"x": ("x", 0), "y": ("blk", 0), "z": ("far", 0), "w": ("far", 1)}


class Hop:
    def __init__(self, number, sizes, steps):
        self.number, self.sizes, self.steps = number, sizes, steps

    def swap(self, values):
        dims = [self.sizes[axis] for axis in AXES]
        pairs = []
        for device in range(math.prod(dims)):
            place, left = [], device
            for size in reversed(dims):
                place.insert(0, left % size)
                left //= size
            axis, bit = self.steps[place[-1]]
            place[AXES.index(axis)] ^= 1 << bit
            target = 0
            for size, coordinate in zip(dims, place):
                target = target * size + coordinate
            pairs.append((device, target))
        return lax.ppermute(values, AXES, pairs)

    def side(self):
        first, second = ((lax.axis_index(axis) >> bit) % 2 for axis, bit in self.steps)
        return jnp.where(lax.axis_index("core") == 0, first, second)


class Hops:
    def __init__(self, sizes):
        self.sizes, self.known = sizes, {}
        self.deep = [("far", bit) for bit in range(2, sizes["far"].bit_length() - 1)]

    def of(self, steps):
        if steps not in self.known:
            self.known[steps] = Hop(len(self.known), self.sizes, steps)
        return self.known[steps]

    def named(self, names):
        found = []
        for name in filter(None, names.split(".")):
            steps = ("core", 0) if name == "c" else None
            pair = (steps, steps) if steps else tuple(BIT_OF[letter] for letter in name)
            found.append(self.of(pair))
        return found

    def rest(self):
        return [self.of((step, step)) for step in self.deep]

    def sides(self):
        return jnp.stack([hop.side() for hop in self.known.values()]).astype(jnp.int32)


class Job:
    def __init__(self, steps):
        self.steps, self.waiting, self.result = steps, None, None
        self.advance()

    def advance(self):
        try:
            hop, values = self.steps.send(self.waiting)
        except StopIteration as stop:
            self.result, self.waiting = stop.value, None
            return
        self.waiting = hop.swap(values)

    def done(self):
        return self.waiting is None


class Part:
    def __init__(self, values, cuts=()):
        self.values, self.cuts = values, cuts

    def cut(self, hop, rows):
        return Part(self.values, self.cuts + ((hop.number, rows),))


def begin_of(sides_ref, cuts, flipped=None):
    total = 0
    for number, rows in cuts:
        total = total + sides_ref[number] * rows
    if flipped is not None:
        number, rows = flipped
        total = total + (1 - sides_ref[number]) * rows
    return total


def add_cost(rows):
    return 0.7 + ADD_SLOPE * rows / 768


def add_call(sides, parts, rows, flipped=None):
    width = parts[0].values.shape[1]
    assert rows % 16 == 0

    def body(sides_ref, *refs):
        total = None
        for ref, part in zip(refs, parts):
            begin = begin_of(sides_ref, part.cuts, flipped)
            if not isinstance(begin, int):
                begin = pl.multiple_of(begin, 16)
            piece = ref[pl.ds(begin, rows), :].astype(F32)
            total = piece if total is None else total + piece
        refs[-1][...] = total.astype(BF16)

    operands = (sides,) + tuple(part.values for part in parts)
    return kernel_call(
        body, "add", [shape((rows, width), BF16)], operands, 16, add_cost(rows), scalars=1
    )[0]


def join_call(sides, hop, mine, other):
    rows, width = mine.shape
    assert rows % 16 == 0

    def body(sides_ref, mine_ref, other_ref, out_ref):
        side = sides_ref[hop.number]
        out_ref[pl.ds(pl.multiple_of(side * rows, 16), rows), :] = mine_ref[...]
        out_ref[pl.ds(pl.multiple_of((1 - side) * rows, 16), rows), :] = other_ref[...]

    outs = [shape((2 * rows, width), BF16)]
    return kernel_call(body, "join", outs, (sides, mine, other), 16, 0.9, scalars=1)[0]


def sum_steps(sides, values, scatter, exchange):
    rows = values.shape[0]
    parts = [Part(values)]
    for hop in scatter:
        rows //= 2
        sent = add_call(sides, parts, rows, (hop.number, rows))
        got = yield hop, sent
        parts = [part.cut(hop, rows) for part in parts] + [Part(got)]
    for hop in exchange:
        whole = add_call(sides, parts, rows)
        got = yield hop, whole
        parts = [Part(whole), Part(got)]
    whole = add_call(sides, parts, rows)
    for hop in reversed(scatter[1:]):
        other = yield hop, whole
        whole = join_call(sides, hop, whole, other)
    other = yield scatter[0], whole
    return whole, other


PLAN = {
    "F0": ("c.xy.wx", "zw.yz"),
    "F1": ("c.zx.xy.yw", "wz"),
    "qk": ("c.yx.xz.zw.wy", ""),
    "rest": ("c.xz.wy", "zx.yw"),
}
SCHEDULE = (
    "ffn0", "F0", "F0", "ffn1", "F1", "out", "F0", "F1",
    "proj_back", "ab0", "F0", "F1", "ab1", "F1", "out", "F0",
    "qw", "qk", "F0", "F1", "qk", "ib", "gin", "rest",
    "qk", "F1", "rest", "qk", "F0", "qk", "F1", "rest",
    "qk", "gin", "qk", "rest", "qk", "F1", "rest", "F0",
    "qk", "rest", "F0", "rest", "qk", "F1", "qk", "rest",
    "F1", "rest",
)


def home_call(sides, hop, kept, back):
    rows = kept.shape[0]

    def body(sides_ref, kept_ref, back_ref, out_ref):
        side = sides_ref[hop.number]
        out_ref[pl.ds(side * rows, rows)] = kept_ref[...]
        out_ref[pl.ds((1 - side) * rows, rows)] = back_ref[...]

    outs = [shape((2 * rows,) + kept.shape[1:], BF16)]
    return kernel_call(body, "home", outs, (sides, kept, back), 16, 1.0, scalars=1)[0]


def home_steps(sides, hop, kept, values):
    back = yield hop, values
    return home_call(sides, hop, kept, back)


def swap_steps(hop, values):
    got = yield hop, values
    return got


def on_device(
    sizes,
    inputs,
    cotangent,
    flags,
    gain_one,
    shift_one,
    query_weight,
    query_bias,
    key_weight,
    value_weight,
    value_bias,
    proj_weight,
    proj_bias,
    gain_two,
    shift_two,
    inner_weight,
    inner_bias,
    outer_weight,
    outer_bias,
):
    batch, half, width = inputs.shape
    hidden = inner_weight.shape[1]
    rows = batch // 2
    assert rows == 2 and sizes["blk"] == 2
    length = 2 * half

    hops = Hops(sizes)
    y_hop = hops.named("yy")[0]
    planned = {
        name: (hops.named(scatter), hops.named(exchange) + hops.rest())
        for name, (scatter, exchange) in PLAN.items()
    }
    sides = hops.sides()

    def row(vector):
        return vector.reshape(1, -1)

    CHAIN.append(Chain())

    blk = lax.axis_index("blk")

    def kept_rows(values):
        return lax.dynamic_slice_in_dim(values, blk * rows, rows, 0)

    def sent_rows(values):
        return lax.dynamic_slice_in_dim(values, (1 - blk) * rows, rows, 0)

    def strides(values):
        return values.reshape(rows, half, -1)

    start = (1 - blk) * rows
    head = lax.dynamic_slice_in_dim(inputs, start, 1, 0)
    inputs, head = lax.optimization_barrier((inputs, head))
    sent = [head[0]] + [
        lax.dynamic_slice_in_dim(inputs, start + n, 1, 0)[0] for n in range(1, rows)
    ]
    arriving = [Job(swap_steps(y_hop, sent[n])) for n in range(rows)]
    kept = kept_rows(inputs)
    owns = [kept[n] for n in range(rows)]

    weights_one = (
        row(gain_one), row(shift_one), query_weight, key_weight, value_weight,
        row(query_bias), row(value_bias),
    )
    others, qs, ks, vs, mixes, levels = [], [], [], [], [], []
    for n in range(rows):
        arriving[n].advance()
        others.append(arriving[n].result)
        q, k, v = qkv_call(owns[n], others[n], *weights_one)
        if n == rows - 1:
            grad_job = Job(swap_steps(y_hop, grad_sent))
        mixed, level = attention_call(q, k, v)
        if n == 0:
            grad_sent, grad_own = mask_call(
                sent_rows(cotangent), kept_rows(cotangent),
                strides(sent_rows(flags)), strides(kept_rows(flags)),
            )
        for kind, values in zip((qs, ks, vs, mixes, levels), (q, k, v, mixed, level)):
            kind.append(values)
    resid, second = proj_call(
        *mixes, *owns, *others, proj_weight, row(proj_bias), row(gain_two), row(shift_two)
    )
    grad_job.advance()
    grads_out = (grad_own, grad_job.result)

    middle = hidden // 2

    weights_two = (inner_weight, row(inner_bias), outer_weight, row(outer_bias))

    made = {}

    def ffn0():
        return ffn_call(True, False, 0, second, *grads_out, *weights_two, resid)

    def ffn1():
        out, gs = made["ffn0"][:2]
        return ffn_call(False, True, 1, second, *grads_out, *weights_two, out, gs)

    def proj_back():
        return proj_back_call(
            made["ffn1"][2], resid, *grads_out, *mixes, proj_weight, row(gain_two)
        )

    def attention_back(n):
        return attention_back_call(
            n * length, qs[n], ks[n], vs[n], mixes[n], made["proj_back"][1], levels[n]
        )

    def qkv_weights():
        return qkv_weights_call(
            *owns, *others, gain_one.reshape(-1, 1), shift_one.reshape(-1, 1), query_weight,
            key_weight, value_weight, made["proj_back"][2], made["proj_back"][3],
            made["ffn0"][3], made["ffn1"][4], *made["ab0"], *made["ab1"],
        )

    def input_back():
        return input_back_call(
            *owns, *others, made["proj_back"][0], query_weight, key_weight, value_weight,
            row(gain_one), *made["ab0"], *made["ab1"],
        )

    kernels = {
        "ffn0": ffn0,
        "ffn1": ffn1,
        "proj_back": proj_back,
        "ab0": lambda: attention_back(0),
        "ab1": lambda: attention_back(1),
        "qw": qkv_weights,
        "ib": input_back,
    }
    starts = {
        "F0": lambda: made["ffn0"][2],
        "F1": lambda: made["ffn1"][3],
        "qk": lambda: made["qw"][0],
        "rest": lambda: made["qw"][1],
    }
    homes = {
        "out": lambda: made["ffn1"][:2],
        "gin": lambda: made["ib"][:2],
    }
    jobs, places = {}, ()

    def step(name):
        nonlocal places
        if name in kernels:
            made[name] = kernels[name]()
        elif name not in jobs:
            if name in homes:
                jobs[name] = Job(home_steps(sides, y_hop, *homes[name]()))
            else:
                values = starts[name]().reshape(-1, width)
                jobs[name] = Job(sum_steps(sides, values, *planned[name]))
        elif not jobs[name].done():
            jobs[name].advance()
            if not jobs[name].done() or name in homes:
                return
            core_number = planned[name][0][0].number
            if name in ("F0", "F1"):
                skip = 0 if name == "F0" else middle // width
                places = place_call(sides, jobs[name], skip, hidden, places, core_number)
            else:
                made[name] = spread_call(sides, jobs[name], core_number)

    for name in SCHEDULE:
        step(name)
    while not all(job.done() for job in jobs.values()):
        for name in jobs:
            step(name)
    CHAIN.pop()
    inner_weight_grad, outer_weight_grad = places
    query_grad, key_grad = made["qk"]
    value_grad, proj_grad, totals = made["rest"]
    return (
        jobs["out"].result,
        jobs["gin"].result,
        totals[0],
        totals[1],
        query_grad,
        totals[6],
        key_grad,
        value_grad,
        totals[7],
        proj_grad,
        totals[4],
        totals[2],
        totals[3],
        inner_weight_grad,
        totals[8 : 8 + hidden // width].reshape(-1),
        outer_weight_grad,
        totals[5],
    )


def solution(mesh):
    sizes = dict(mesh.shape)
    far = sizes["dp"] // 4
    fine = Mesh(mesh.devices.reshape(sizes["blk"], far, 2, 2), ("blk", "far", "x", "core"))
    rows = ("far", "x", "core")
    split = P(rows, "blk", None)
    in_specs = (split, split, P(rows, "blk")) + (P(),) * 15
    out_specs = (split, split) + (P(),) * 15
    return jax.shard_map(
        functools.partial(on_device, dict(fine.shape)),
        mesh=fine,
        in_specs=in_specs,
        out_specs=out_specs,
        check_vma=False,
    )
```

```python
import functools
import math

import jax
import jax.numpy as jnp
from jax import lax
from jax.experimental import pallas as pl
from jax.experimental.pallas import tpu as pltpu
from jax.sharding import Mesh, PartitionSpec as P

EPS = 1e-05
F32 = jnp.float32
BF16 = jnp.bfloat16
PAIR = 128
MIB = 1024 * 1024
ROOT_HALF = 0.7071067811865476
ROOT_TWO_PI = 0.3989422804014327
VM = pl.BlockSpec(memory_space=pltpu.VMEM)
TILES = 2
FFN_LIMIT = 15


def dot(left, right):
    return lax.dot_general(left, right, (((1,), (0,)), ((), ())), preferred_element_type=F32)


def dot_nt(left, right):
    return lax.dot_general(left, right, (((1,), (1,)), ((), ())), preferred_element_type=F32)


def dot_tn(left, right):
    return lax.dot_general(left, right, (((0,), (0,)), ((), ())), preferred_element_type=F32)


def normalize(values):
    center = values - jnp.mean(values, axis=-1, keepdims=True)
    scale = lax.rsqrt(jnp.mean(center * center, axis=-1, keepdims=True) + EPS)
    return center * scale, scale


def norm_back(grad, unit, scale, gain):
    scaled = grad * gain
    return scale * (
        scaled
        - jnp.mean(scaled, axis=-1, keepdims=True)
        - unit * jnp.mean(scaled * unit, axis=-1, keepdims=True)
    )


def both(one_ref, two_ref):
    return jnp.concatenate([one_ref[...], two_ref[...]], axis=0)


def four(own_ref, other_ref):
    return jnp.concatenate([own_ref[0], other_ref[0], own_ref[1], other_ref[1]], axis=0)


def column_sum(values):
    return jnp.sum(values.astype(F32), axis=0, keepdims=True)


def shape(dims, dtype):
    return jax.ShapeDtypeStruct(dims, dtype)


class Chain:
    def __init__(self):
        self.token = jnp.zeros((8, PAIR), F32)


CHAIN = []
SHARE = 10.0
ADD_SLOPE = 1.2
BYTES = 200.0


def cost_of(us):
    flops, size = int(us * SHARE * 1.15e9), int(us * BYTES * 3.3e6)
    return pl.CostEstimate(flops=flops, bytes_accessed=size, transcendentals=0)


def kernel_call(body, name, outs, operands, limit, us, aliases=(), scalars=0, cut=None):
    chain = CHAIN[-1]
    count = len(operands)

    def whole(*refs):
        body(*refs[:count], *refs[count + 1 : -1])
        refs[-1][...] = jnp.zeros((8, PAIR), F32)

    specs = [pl.BlockSpec(memory_space=pltpu.SMEM)] * scalars + [VM] * (count + 1 - scalars)
    for place, spec in (cut or {}).items():
        specs[place] = spec
    results = pl.pallas_call(
        whole,
        grid=(1,) if cut else (),
        in_specs=specs,
        out_specs=[VM] * (len(outs) + 1),
        out_shape=list(outs) + [shape((8, PAIR), F32)],
        input_output_aliases=dict(aliases),
        compiler_params=pltpu.CompilerParams(vmem_limit_bytes=limit * MIB),
        cost_estimate=cost_of(us),
        name=name,
    )(*operands, chain.token)
    chain.token = results[-1]
    return results[:-1]


def qkv_kernel(own_ref, other_ref, gain, shift, wq, wk, wv, bq, bv, q_ref, k_ref, v_ref):
    unit, _ = normalize(both(own_ref, other_ref).astype(F32))
    first = (unit * gain[...] + shift[...]).astype(BF16)
    q_ref[...] = ((dot(first, wq[...]) + bq[...]).astype(BF16).astype(F32) * 0.125).astype(BF16)
    k_ref[...] = dot(first, wk[...]).astype(BF16)
    v_ref[...] = (dot(first, wv[...]) + bv[...]).astype(BF16)


def qkv_call(own, other, *weights):
    half, width = own.shape
    outs = [shape((2 * half, width), BF16)] * 3
    return kernel_call(
        qkv_kernel, "qkv", outs, (own, other) + weights, 16, 3.0
    )


def mask_kernel(sent_ref, kept_ref, sent_flags, kept_flags, sent_out, kept_out):
    for values, flags, out in ((sent_ref, sent_flags, sent_out), (kept_ref, kept_flags, kept_out)):
        keep = jnp.max(flags[...], axis=-1, keepdims=True)
        out[...] = (values[...].astype(F32) * keep.astype(F32)).astype(BF16)


def mask_call(sent, kept, sent_flags, kept_flags):
    outs = [shape(sent.shape, BF16)] * 2
    return kernel_call(mask_kernel, "mask", outs, (sent, kept, sent_flags, kept_flags), 16, 1.3)


def head_masks():
    lane = lax.broadcasted_iota(jnp.int32, (1, PAIR), 1)
    low = (lane < PAIR // 2).astype(F32)
    return low, 1.0 - low


def masked(values, mask):
    return (values.astype(F32) * mask).astype(BF16)


def attention_kernel(q_ref, k_ref, v_ref, mixed_ref, level_ref):
    length, width = q_ref.shape
    ones = jnp.ones((length, PAIR), BF16)
    masks = head_masks()
    lane = lax.broadcasted_iota(jnp.int32, (1, PAIR), 1)
    levels = jnp.zeros((length, PAIR), F32)
    for pair in range(width // PAIR):
        cols = slice(pair * PAIR, (pair + 1) * PAIR)
        q, k, v = q_ref[:, cols], k_ref[:, cols], v_ref[:, cols]
        wide = jnp.concatenate([v, ones], axis=1)
        total = None
        for head, mask in enumerate(masks):
            scores = dot_nt(masked(q, mask), k)
            top = jnp.max(scores, axis=-1, keepdims=True)
            weights = jnp.exp(scores - top).astype(BF16)
            sums = dot(weights, wide)
            part = sums[:, :PAIR] * ((1.0 / sums[:, PAIR:]) * mask)
            total = part if total is None else total + part
            levels = jnp.where(lane == 2 * pair + head, top + jnp.log(sums[:, PAIR:]), levels)
        mixed_ref[:, cols] = total.astype(BF16)
    level_ref[...] = levels


def attention_call(q, k, v):
    length, width = q.shape
    outs = [shape((length, width), BF16), shape((length, PAIR), F32)]
    return kernel_call(
        attention_kernel, "attention", outs, (q, k, v), 16, 4.7
    )


def attention_back_kernel(begin, q_ref, k_ref, v_ref, mixed_ref, grad_ref, level_ref,
                          dq_ref, dk_ref, dv_ref):
    length, width = q_ref.shape
    masks = head_masks()
    half = PAIR // 2
    for pair in range(width // PAIR):
        cols = slice(pair * PAIR, (pair + 1) * PAIR)
        q, k, v = q_ref[:, cols], k_ref[:, cols], v_ref[:, cols]
        grad = grad_ref[begin : begin + length, cols]
        dots = grad.astype(F32) * mixed_ref[:, cols].astype(F32)
        grad_t = grad.T
        q_t = q.T
        dq = None
        dk, dv = [], []
        for head, mask in enumerate(masks):
            place = 2 * pair + head
            probs = jnp.exp(dot_nt(masked(q, mask), k) - level_ref[:, place : place + 1])
            grad_probs = dot_nt(masked(grad, mask), v)
            delta = jnp.sum(dots * mask, axis=-1, keepdims=True)
            scores = (probs * (grad_probs - delta)).astype(BF16)
            part = dot(scores, masked(k, mask))
            dq = part if dq is None else dq + part
            rows = slice(head * half, (head + 1) * half)
            dv.append(dot(grad_t, probs.astype(BF16))[rows])
            dk.append(dot(q_t, scores)[rows])
        dq_ref[:, cols] = (dq * 0.125).astype(BF16)
        dk_ref[:, cols] = jnp.concatenate(dk, axis=0).T.astype(BF16)
        dv_ref[:, cols] = jnp.concatenate(dv, axis=0).T.astype(BF16)


def attention_back_call(begin, q, k, v, mixed, grad, levels):
    length, width = q.shape
    outs = [shape((length, width), BF16)] * 3
    return kernel_call(
        functools.partial(attention_back_kernel, begin),
        "attention_back", outs, (q, k, v, mixed, grad, levels), 16, 7.8,
    )


def proj_kernel(mixed_one, mixed_two, own_one, own_two, other_one, other_two, w, b, gain, shift,
                resid_ref, second_ref):
    half = mixed_one.shape[0]
    rows_of = ((mixed_one, own_one, other_one), (mixed_two, own_two, other_two))
    for n, (mixed, own, other) in enumerate(rows_of):
        rows = slice(n * half, (n + 1) * half)
        resid = both(own, other).astype(F32) + (dot(mixed[...], w[...]) + b[...])
        resid_ref[rows, :] = resid
        unit, _ = normalize(resid)
        second_ref[rows, :] = (unit * gain[...] + shift[...]).astype(BF16)


def proj_call(*operands):
    half, width = operands[0].shape
    outs = [shape((2 * half, width), F32), shape((2 * half, width), BF16)]
    return kernel_call(proj_kernel, "proj", outs, operands, 16, 3.1)


def ffn_kernel(start, last, tiles, second_ref, grad_own, grad_other, w_in, b_in, w_out, b_out, base_ref, *refs):
    if start:
        out_ref, gs_ref, dw_ref, dbias_ref = refs
    else:
        more_ref, own_ref, other_ref, gs_ref, dw_ref, dbias_ref = refs
    tokens, width = second_ref.shape
    half = tokens // 4
    count = tokens // tiles
    for m in range(tiles):
        rows = slice(m * count, (m + 1) * count)
        second = second_ref[rows, :]
        pieces = [(n // 2, n % 2) for n in range(4)][m * 4 // tiles : (m + 1) * 4 // tiles]
        grad = jnp.concatenate(
            [(grad_other if side else grad_own)[n] for n, side in pieces], axis=0
        )
        out = base_ref[rows, :]
        gs = None if start else more_ref[rows, :]
        for n in range(w_in.shape[1] // width):
            cols = slice(n * width, (n + 1) * width)
            inner = dot(second, w_in[:, cols]) + b_in[:, cols]
            dact = dot_nt(grad, w_out[cols, :])
            phi = 0.5 * (1.0 + lax.erf(inner * ROOT_HALF))
            act = (inner * phi).astype(BF16)
            slope = phi + inner * jnp.exp(-0.5 * inner * inner) * ROOT_TWO_PI
            ginner = (dact * slope).astype(BF16)
            out = out + dot(act, w_out[cols, :])
            more = dot_nt(ginner, w_in[:, cols])
            gs = more if gs is None else gs + more
            d_out = dot_tn(act, grad)
            d_in = dot_tn(second, ginner)
            bias = column_sum(ginner)
            if m > 0:
                d_out = d_out + dw_ref[n, 1].astype(F32)
                d_in = d_in + dw_ref[n, 0].astype(F32)
                bias = bias + dbias_ref[:, cols]
            dw_ref[n, 1] = d_out.astype(BF16)
            dw_ref[n, 0] = d_in.astype(BF16)
            dbias_ref[:, cols] = bias
        gs_ref[rows, :] = gs
        if last:
            low = (out + b_out[...]).astype(BF16)
            for place, (row, side) in enumerate(pieces):
                (other_ref if side else own_ref)[row] = low[place * half : (place + 1) * half]
        else:
            out_ref[rows, :] = out


def ffn_call(start, last, number, *operands):
    tokens, width = operands[0].shape
    span = operands[3].shape[1] // 2
    pieces = [shape((2, tokens // 4, width), BF16)] * 2
    outs = (pieces if last else [shape((tokens, width), F32)]) + [
        shape((tokens, width), F32),
        shape((span // width, 2, width, width), BF16),
        shape((1, span), F32),
    ]
    once = pl.Buffered(1)
    cut = {
        3: pl.BlockSpec((width, span), lambda i: (0, number), pipeline_mode=once),
        4: pl.BlockSpec((1, span), lambda i: (0, number), pipeline_mode=once),
        5: pl.BlockSpec((span, width), lambda i: (number, 0), pipeline_mode=once),
    }
    return kernel_call(
        functools.partial(ffn_kernel, start, last, TILES),
        "ffn", outs, operands, FFN_LIMIT, 18.0, () if start else ((8, 2 if last else 1),),
        cut=cut,
    )


def proj_back_kernel(gs_ref, resid_ref, grad_own, grad_other, mixed_one, mixed_two, w, gain,
                     gresid_ref, gmixed_ref, dw_ref, vec_ref):
    unit, scale = normalize(resid_ref[...])
    gs = gs_ref[...]
    grad = four(grad_own, grad_other).astype(F32)
    gresid = grad + norm_back(gs, unit, scale, gain[...])
    gresid_ref[...] = gresid
    branch = gresid.astype(BF16)
    gmixed_ref[...] = dot_nt(branch, w[...]).astype(BF16)
    dw_ref[...] = dot_tn(both(mixed_one, mixed_two), branch).astype(BF16)
    sums = (column_sum(gs * unit), column_sum(gs), column_sum(branch), column_sum(grad))
    for n, total in enumerate(sums):
        vec_ref[n : n + 1, :] = total


def proj_back_call(*operands):
    tokens, width = operands[0].shape
    outs = [
        shape((tokens, width), F32),
        shape((tokens, width), BF16),
        shape((width, width), BF16),
        shape((4, width), F32),
    ]
    return kernel_call(
        proj_back_kernel, "proj_back", outs, operands, 24, 6.0, ((0, 0),)
    )


VECTOR_ROWS = 64


def qkv_weights_kernel(own_one, own_two, other_one, other_two, gain, shift, wq, wk, wv,
                       dw_proj, vec_two, bias_one, bias_two, *refs):
    dw_ref, rest_ref = refs[6:]
    width = own_one.shape[1]
    units = [
        normalize(both(own, other).astype(F32))[0].astype(BF16)
        for own, other in ((own_one, other_one), (own_two, other_two))
    ]
    unit = jnp.concatenate(units, axis=0)
    gains, shifts = gain[...], shift[...]
    sums, by_gain, by_shift = [], None, None
    for n, w in enumerate((wq, wk, wv)):
        grad = both(refs[n], refs[3 + n])
        terms = dot_tn(unit, grad)
        total = column_sum(grad)
        weight = w[...].astype(F32)
        dw = (terms * gains + shifts * total).astype(BF16)
        if n < 2:
            dw_ref[n] = dw
        else:
            rest_ref[0, :width, :] = dw
        gained, shifted = weight * terms, weight * total
        by_gain = gained if by_gain is None else by_gain + gained
        by_shift = shifted if by_shift is None else by_shift + shifted
        sums.append(total)
    lane = lax.broadcasted_iota(jnp.int32, (1, PAIR), 1)
    columns = jnp.where(
        lane == 0,
        jnp.sum(by_gain, axis=-1, keepdims=True),
        jnp.sum(by_shift, axis=-1, keepdims=True),
    )
    vectors = [columns.T[:2], vec_two[...], sums[0], sums[2]]
    for bias in (bias_one, bias_two):
        for n in range(bias.shape[1] // width):
            vectors.append(bias[:, n * width : (n + 1) * width])
    count = sum(part.shape[0] for part in vectors)
    vectors.append(jnp.zeros((VECTOR_ROWS - count, width), F32))
    rest_ref[0, width:, :] = jnp.concatenate(vectors, axis=0).astype(BF16)
    rest_ref[1, :width, :] = dw_proj[...]
    rest_ref[1, width:, :] = jnp.zeros((VECTOR_ROWS, width), BF16)


def qkv_weights_call(*operands):
    length, width = operands[-1].shape
    outs = [
        shape((2, width, width), BF16), shape((2, width + VECTOR_ROWS, width), BF16),
    ]
    return kernel_call(qkv_weights_kernel, "qkv_weights", outs, operands, 24, 6.5)


def input_back_kernel(own_one, own_two, other_one, other_two, gresid_ref, wq, wk, wv, gain, *refs):
    own_ref, other_ref = refs[6:]
    half = own_one.shape[0]
    for n, (own, other) in enumerate(((own_one, other_one), (own_two, other_two))):
        dq, dk, dv = refs[3 * n : 3 * n + 3]
        gfirst = dot_nt(dq[...], wq[...]) + dot_nt(dk[...], wk[...]) + dot_nt(dv[...], wv[...])
        unit, scale = normalize(both(own, other).astype(F32))
        rows = slice(2 * n * half, 2 * (n + 1) * half)
        gin = gresid_ref[rows, :] + norm_back(gfirst, unit, scale, gain[...])
        own_ref[n] = gin[:half].astype(BF16)
        other_ref[n] = gin[half:].astype(BF16)


def input_back_call(*operands):
    half, width = operands[0].shape
    outs = [shape((2, half, width), BF16)] * 2
    return kernel_call(input_back_kernel, "input_back", outs, operands, 16, 6.2)


CHUNKS = 4


def place_call(sides, part, flipped, skip, hidden, earlier, core_number):
    chain = CHAIN[-1]
    width = part.shape[1]
    rows = width // CHUNKS

    def block(sides_ref):
        side = sides_ref[core_number]
        return skip + (1 - side if flipped else side)

    def body(sides_ref, part_ref, *refs):
        inner_ref, outer_ref, token_ref = refs[-3:]
        here = pl.program_id(0) * rows
        first = pl.ds(pl.multiple_of(here, 16), rows)
        second = pl.ds(pl.multiple_of(width + here, 16), rows)
        inner_ref[...] = part_ref[first, :].astype(F32)
        outer_ref[...] = part_ref[second, :].astype(F32)
        token_ref[...] = jnp.zeros((8, PAIR), F32)

    results = pl.pallas_call(
        body,
        grid_spec=pltpu.PrefetchScalarGridSpec(
            num_scalar_prefetch=1,
            grid=(CHUNKS,),
            in_specs=[VM] * 2 + [pl.BlockSpec(memory_space=pl.ANY)] * len(earlier),
            out_specs=[
                pl.BlockSpec((rows, width), lambda c, ref: (c, block(ref))),
                pl.BlockSpec((rows, width), lambda c, ref: (block(ref) * CHUNKS + c, 0)),
                VM,
            ],
        ),
        out_shape=[
            shape((width, hidden), F32), shape((hidden, width), F32), shape((8, PAIR), F32),
        ],
        input_output_aliases={3 + n: n for n in range(len(earlier))},
        compiler_params=pltpu.CompilerParams(vmem_limit_bytes=8 * MIB),
        cost_estimate=cost_of(2.7),
        name="place",
    )(sides, part, chain.token, *earlier)
    chain.token = results[-1]
    return results[:-1]


def spread_call(sides, job, core_number):
    chain = CHAIN[-1]
    operands = job.result
    total, width = operands[0].shape
    rows = width // CHUNKS
    more = total - width

    def body(sides_ref, mine_ref, other_ref, token_in, low_ref, high_ref, *refs):
        here = pl.ds(pl.multiple_of(pl.program_id(0) * rows, 16), rows)
        for side in range(2):
            low, high = (mine_ref, other_ref) if side == 0 else (other_ref, mine_ref)

            @pl.when(sides_ref[core_number] == side)
            def _():
                low_ref[...] = low[here, :].astype(F32)
                high_ref[...] = high[here, :].astype(F32)
                if more:
                    refs[0][...] = low[width:, :].astype(F32)

        refs[-1][...] = jnp.zeros((8, PAIR), F32)

    part = pl.BlockSpec((rows, width), lambda c: (c, 0))
    results = pl.pallas_call(
        body,
        grid=(CHUNKS,),
        in_specs=[pl.BlockSpec(memory_space=pltpu.SMEM)] + [VM] * 3,
        out_specs=[part, part] + [VM] * (2 if more else 1),
        out_shape=[shape((width, width), F32)] * 2
        + ([shape((more, width), F32)] if more else [])
        + [shape((8, PAIR), F32)],
        compiler_params=pltpu.CompilerParams(vmem_limit_bytes=8 * MIB),
        cost_estimate=cost_of(3.0),
        name="spread",
    )(sides, *operands, chain.token)
    chain.token = results[-1]
    return results[:-1]


AXES = ("blk", "far", "x", "core")
BIT_OF = {"x": ("x", 0), "y": ("blk", 0), "z": ("far", 0), "w": ("far", 1)}


class Hop:
    def __init__(self, number, sizes, steps):
        self.number, self.sizes, self.steps = number, sizes, steps

    def swap(self, values):
        dims = [self.sizes[axis] for axis in AXES]
        pairs = []
        for device in range(math.prod(dims)):
            place, left = [], device
            for size in reversed(dims):
                place.insert(0, left % size)
                left //= size
            axis, bit = self.steps[place[-1]]
            place[AXES.index(axis)] ^= 1 << bit
            target = 0
            for size, coordinate in zip(dims, place):
                target = target * size + coordinate
            pairs.append((device, target))
        return lax.ppermute(values, AXES, pairs)

    def side(self):
        first, second = ((lax.axis_index(axis) >> bit) % 2 for axis, bit in self.steps)
        return jnp.where(lax.axis_index("core") == 0, first, second)


class Hops:
    def __init__(self, sizes):
        self.sizes, self.known = sizes, {}
        self.deep = [("far", bit) for bit in range(2, sizes["far"].bit_length() - 1)]

    def of(self, steps):
        if steps not in self.known:
            self.known[steps] = Hop(len(self.known), self.sizes, steps)
        return self.known[steps]

    def named(self, names):
        found = []
        for name in filter(None, names.split(".")):
            steps = ("core", 0) if name == "c" else None
            pair = (steps, steps) if steps else tuple(BIT_OF[letter] for letter in name)
            found.append(self.of(pair))
        return found

    def rest(self):
        return [self.of((step, step)) for step in self.deep]

    def sides(self):
        return jnp.stack([hop.side() for hop in self.known.values()]).astype(jnp.int32)


class Job:
    def __init__(self, steps):
        self.steps, self.waiting, self.result = steps, None, None
        self.advance()

    def advance(self):
        try:
            hop, values = self.steps.send(self.waiting)
        except StopIteration as stop:
            self.result, self.waiting = stop.value, None
            return
        self.waiting = hop.swap(values)

    def done(self):
        return self.waiting is None


class Part:
    def __init__(self, values, cuts=()):
        self.values, self.cuts = values, cuts

    def cut(self, hop, rows):
        return Part(self.values, self.cuts + ((hop.number, rows),))


def begin_of(sides_ref, cuts, flipped=None):
    total = 0
    for number, rows in cuts:
        total = total + sides_ref[number] * rows
    if flipped is not None:
        number, rows = flipped
        total = total + (1 - sides_ref[number]) * rows
    return total


def add_cost(rows):
    return 0.7 + ADD_SLOPE * rows / 768


def add_call(sides, parts, rows, flipped=None):
    width = parts[0].values.shape[1]
    assert rows % 16 == 0

    def body(sides_ref, *refs):
        total = None
        for ref, part in zip(refs, parts):
            begin = begin_of(sides_ref, part.cuts, flipped)
            if not isinstance(begin, int):
                begin = pl.multiple_of(begin, 16)
            piece = ref[pl.ds(begin, rows), :].astype(F32)
            total = piece if total is None else total + piece
        refs[-1][...] = total.astype(BF16)

    operands = (sides,) + tuple(part.values for part in parts)
    return kernel_call(
        body, "add", [shape((rows, width), BF16)], operands, 16, add_cost(rows), scalars=1
    )[0]


def join_call(sides, hop, mine, other):
    rows, width = mine.shape
    assert rows % 16 == 0

    def body(sides_ref, mine_ref, other_ref, out_ref):
        side = sides_ref[hop.number]
        out_ref[pl.ds(pl.multiple_of(side * rows, 16), rows), :] = mine_ref[...]
        out_ref[pl.ds(pl.multiple_of((1 - side) * rows, 16), rows), :] = other_ref[...]

    outs = [shape((2 * rows, width), BF16)]
    return kernel_call(body, "join", outs, (sides, mine, other), 16, 0.9, scalars=1)[0]


def sum_steps(sides, values, scatter, exchange, ready=None):
    rows = values.shape[0]
    parts = [Part(values)]
    for hop in scatter:
        rows //= 2
        sent = add_call(sides, parts, rows, (hop.number, rows))
        got = yield hop, sent
        parts = [part.cut(hop, rows) for part in parts] + [Part(got)]
    for hop in exchange:
        whole = add_call(sides, parts, rows)
        got = yield hop, whole
        parts = [Part(whole), Part(got)]
    whole = add_call(sides, parts, rows)
    for hop in reversed(scatter[1:]):
        other = yield hop, whole
        whole = join_call(sides, hop, whole, other)
    if ready is not None:
        ready(whole, False)
    other = yield scatter[0], whole
    if ready is not None:
        ready(other, True)
    return whole, other


PLAN = {
    "F0": ("c.xy.wx", "zw.yz"),
    "F1": ("c.zx.xy.yw", "wz"),
    "qk": ("c.yx.xz.zw.wy", ""),
    "rest": ("c.xz.wy", "zx.yw"),
}
SCHEDULE = (
    "ffn0", "F0", "F0", "ffn1", "F1", "out", "F0", "F1",
    "proj_back", "ab0", "F0", "F1", "ab1", "F1", "out", "F0",
    "qw", "qk", "F0", "F1", "qk", "ib", "gin", "rest",
    "qk", "F1", "rest", "qk", "F0", "qk", "F1", "rest",
    "qk", "gin", "qk", "rest", "qk", "F1", "rest", "F0",
    "qk", "rest", "F0", "rest", "qk", "F1", "qk", "rest",
    "F1", "rest",
)


def home_call(sides, hop, kept, back):
    rows = kept.shape[0]

    def body(sides_ref, kept_ref, back_ref, out_ref):
        side = sides_ref[hop.number]
        out_ref[pl.ds(side * rows, rows)] = kept_ref[...]
        out_ref[pl.ds((1 - side) * rows, rows)] = back_ref[...]

    outs = [shape((2 * rows,) + kept.shape[1:], BF16)]
    return kernel_call(body, "home", outs, (sides, kept, back), 16, 1.0, scalars=1)[0]


def home_steps(sides, hop, kept, values):
    back = yield hop, values
    return home_call(sides, hop, kept, back)


def swap_steps(hop, values):
    got = yield hop, values
    return got


def on_device(
    sizes,
    inputs,
    cotangent,
    flags,
    gain_one,
    shift_one,
    query_weight,
    query_bias,
    key_weight,
    value_weight,
    value_bias,
    proj_weight,
    proj_bias,
    gain_two,
    shift_two,
    inner_weight,
    inner_bias,
    outer_weight,
    outer_bias,
):
    batch, half, width = inputs.shape
    hidden = inner_weight.shape[1]
    rows = batch // 2
    assert rows == 2 and sizes["blk"] == 2
    length = 2 * half

    hops = Hops(sizes)
    y_hop = hops.named("yy")[0]
    planned = {
        name: (hops.named(scatter), hops.named(exchange) + hops.rest())
        for name, (scatter, exchange) in PLAN.items()
    }
    sides = hops.sides()

    def row(vector):
        return vector.reshape(1, -1)

    CHAIN.append(Chain())

    blk = lax.axis_index("blk")

    def kept_rows(values):
        return lax.dynamic_slice_in_dim(values, blk * rows, rows, 0)

    def sent_rows(values):
        return lax.dynamic_slice_in_dim(values, (1 - blk) * rows, rows, 0)

    def strides(values):
        return values.reshape(rows, half, -1)

    start = (1 - blk) * rows
    head = lax.dynamic_slice_in_dim(inputs, start, 1, 0)
    inputs, head = lax.optimization_barrier((inputs, head))
    sent = [head[0]] + [
        lax.dynamic_slice_in_dim(inputs, start + n, 1, 0)[0] for n in range(1, rows)
    ]
    arriving = [Job(swap_steps(y_hop, sent[n])) for n in range(rows)]
    kept = kept_rows(inputs)
    owns = [kept[n] for n in range(rows)]

    weights_one = (
        row(gain_one), row(shift_one), query_weight, key_weight, value_weight,
        row(query_bias), row(value_bias),
    )
    others, qs, ks, vs, mixes, levels = [], [], [], [], [], []
    for n in range(rows):
        arriving[n].advance()
        others.append(arriving[n].result)
        q, k, v = qkv_call(owns[n], others[n], *weights_one)
        if n == rows - 1:
            grad_job = Job(swap_steps(y_hop, grad_sent))
        mixed, level = attention_call(q, k, v)
        if n == 0:
            grad_sent, grad_own = mask_call(
                sent_rows(cotangent), kept_rows(cotangent),
                strides(sent_rows(flags)), strides(kept_rows(flags)),
            )
        for kind, values in zip((qs, ks, vs, mixes, levels), (q, k, v, mixed, level)):
            kind.append(values)
    resid, second = proj_call(
        *mixes, *owns, *others, proj_weight, row(proj_bias), row(gain_two), row(shift_two)
    )
    grad_job.advance()
    grads_out = (grad_own, grad_job.result)

    middle = hidden // 2

    weights_two = (inner_weight, row(inner_bias), outer_weight, row(outer_bias))

    made = {}

    def ffn0():
        return ffn_call(True, False, 0, second, *grads_out, *weights_two, resid)

    def ffn1():
        out, gs = made["ffn0"][:2]
        return ffn_call(False, True, 1, second, *grads_out, *weights_two, out, gs)

    def proj_back():
        return proj_back_call(
            made["ffn1"][2], resid, *grads_out, *mixes, proj_weight, row(gain_two)
        )

    def attention_back(n):
        return attention_back_call(
            n * length, qs[n], ks[n], vs[n], mixes[n], made["proj_back"][1], levels[n]
        )

    def qkv_weights():
        return qkv_weights_call(
            *owns, *others, gain_one.reshape(-1, 1), shift_one.reshape(-1, 1), query_weight,
            key_weight, value_weight, made["proj_back"][2], made["proj_back"][3],
            made["ffn0"][3], made["ffn1"][4], *made["ab0"], *made["ab1"],
        )

    def input_back():
        return input_back_call(
            *owns, *others, made["proj_back"][0], query_weight, key_weight, value_weight,
            row(gain_one), *made["ab0"], *made["ab1"],
        )

    kernels = {
        "ffn0": ffn0,
        "ffn1": ffn1,
        "proj_back": proj_back,
        "ab0": lambda: attention_back(0),
        "ab1": lambda: attention_back(1),
        "qw": qkv_weights,
        "ib": input_back,
    }
    starts = {
        "F0": lambda: made["ffn0"][2],
        "F1": lambda: made["ffn1"][3],
        "qk": lambda: made["qw"][0],
        "rest": lambda: made["qw"][1],
    }
    homes = {
        "out": lambda: made["ffn1"][:2],
        "gin": lambda: made["ib"][:2],
    }
    jobs, places = {}, ()

    def put(name, part, flipped):
        nonlocal places
        skip = 0 if name == "F0" else middle // width
        core_number = planned[name][0][0].number
        places = place_call(sides, part, flipped, skip, hidden, places, core_number)

    def step(name):
        if name in kernels:
            made[name] = kernels[name]()
        elif name not in jobs:
            if name in homes:
                jobs[name] = Job(home_steps(sides, y_hop, *homes[name]()))
            else:
                values = starts[name]().reshape(-1, width)
                ready = functools.partial(put, name) if name in ("F0", "F1") else None
                jobs[name] = Job(sum_steps(sides, values, *planned[name], ready))
        elif not jobs[name].done():
            jobs[name].advance()
            if not jobs[name].done() or name in homes:
                return
            if name not in ("F0", "F1"):
                made[name] = spread_call(sides, jobs[name], planned[name][0][0].number)

    for name in SCHEDULE:
        step(name)
    while not all(job.done() for job in jobs.values()):
        for name in jobs:
            step(name)
    CHAIN.pop()
    inner_weight_grad, outer_weight_grad = places
    query_grad, key_grad = made["qk"]
    value_grad, proj_grad, totals = made["rest"]
    return (
        jobs["out"].result,
        jobs["gin"].result,
        totals[0],
        totals[1],
        query_grad,
        totals[6],
        key_grad,
        value_grad,
        totals[7],
        proj_grad,
        totals[4],
        totals[2],
        totals[3],
        inner_weight_grad,
        totals[8 : 8 + hidden // width].reshape(-1),
        outer_weight_grad,
        totals[5],
    )


def solution(mesh):
    sizes = dict(mesh.shape)
    far = sizes["dp"] // 4
    fine = Mesh(mesh.devices.reshape(sizes["blk"], far, 2, 2), ("blk", "far", "x", "core"))
    rows = ("far", "x", "core")
    split = P(rows, "blk", None)
    in_specs = (split, split, P(rows, "blk")) + (P(),) * 15
    out_specs = (split, split) + (P(),) * 15
    return jax.shard_map(
        functools.partial(on_device, dict(fine.shape)),
        mesh=fine,
        in_specs=in_specs,
        out_specs=out_specs,
        check_vma=False,
    )
```
